256 devices in a mesh: row: 8 (over y, core), col: 32 (over z, x).
Axes of the slice: x: 4, y: 4, z: 8, core: 2. Of those that a mesh axis runs over, the one named last changes fastest.
Arguments:
- embeddings: bfloat16 [64, 65536], P(None, ('row', 'col')), may hold values from -6 to 6
- latent: float32 [65536], P(('row', 'col')), may hold values from -162 to 162
- list_of: int32 [65536], P(('row', 'col')), may hold values from 0 to 8191, as said below
- rank_of: int32 [65536], P(('row', 'col')), may hold values from 0 to 7, as said below
- probes: float32 [15, 65536], P(None, ('row', 'col')), may hold values from -6 to 6
Outputs:
- solution: float32 [16, 65536], P(None, ('row', 'col'))
- residual: float32 [16, 65536], P(None, ('row', 'col'))
The draws below stay inside these ranges and needn't reach their ends.
Inputs may be any that keep to these rules, and one draw needn't show every extreme that they name: `list_of`: the 8 members of every list lie in one aligned block of 256 consecutive completions; every list has exactly 8 members. `rank_of`: within each list the places are 0 to 7, each once.
All inputs are finite; a program needn't handle non-finite values.
Results may differ from the reference program's by a relative error of at most 0.008.
Values may be sent and summed in bfloat16 or wider, within the bound.
No kernel may reach another device: no remote copies, remote signals or barrier semaphores. Data moves between devices by JAX's collectives and lax.ppermute only.
A program may use at most 64 MiB of HBM per device.

```python
import jax
import jax.numpy as jnp
from jax import lax

D = 64
SIDES = 16
ITERS = 2
LIST_LEN = 8
PT_DEV = 256
N = 65536
LISTS = 8192


def block_orders(key):
    values = jax.random.permutation(key, N).reshape(N // PT_DEV, PT_DEV)
    first = jnp.argsort(values, axis=1, stable=True)
    return jnp.argsort(first, axis=1, stable=True).astype(jnp.int32)


def draw_list_of(key, part):
    local = block_orders(key)
    base = (jnp.arange(N // PT_DEV, dtype=jnp.int32) * (PT_DEV // LIST_LEN))[:, None]
    return (base + local // LIST_LEN).reshape(N)


def draw_rank_of(key, part):
    local = block_orders(key)
    key = jax.random.fold_in(key, 2)
    order = block_orders(key)
    groups = local // LIST_LEN
    same_list = groups[:, :, None] == groups[:, None, :]
    before = order[:, None, :] < order[:, :, None]
    return jnp.sum((same_list & before).astype(jnp.int32), axis=2).reshape(N)


def draw_latent(key, part):
    key = jax.random.fold_in(key, 3)
    key_base = jax.random.fold_in(key, 0)
    values = jnp.clip(2.0 * jax.random.normal(key_base, (N,), jnp.float32), -12.0, 12.0)
    return values


def steps_of(own_key, extent, pieces, least, high):
    gain, own = 1.0, jax.random.fold_in(own_key, 6)
    for dim, shards_of in pieces:
        draws = jnp.exp(jax.random.uniform(jax.random.fold_in(own, dim), (shards_of,), jnp.float32, least / len(pieces), high / len(pieces)))
        gain = gain * jnp.repeat(draws, extent[dim] // shards_of).reshape([-1 if axis == dim else 1 for axis in range(len(extent))])
    return gain


def scatter_about(key, shape, scale, bound, pieces=(), kind=jnp.bfloat16):
    factor_of = steps_of(key, shape, pieces, -0.22, 0.18) if pieces else 1.0
    values = jax.random.normal(key, shape, jnp.float32) * scale * factor_of
    return jnp.minimum(jnp.maximum(values, -bound), bound).astype(kind)


def setup_inputs(seed: int = 0) -> dict:
    key_of = jax.random.split(jax.random.key(seed), 6)
    embeddings = scatter_about(key_of[0], (D, N), 1.0, 6.0, ((1, 256),))
    latent = draw_latent(jax.random.fold_in(key_of[5], 71), 0)
    list_of = draw_list_of(jax.random.fold_in(key_of[5], 71), 0)
    rank_of = draw_rank_of(jax.random.fold_in(key_of[5], 71), 0)
    probes = scatter_about(key_of[4], (SIDES - 1, N), 1.0, 6.0, ((1, 256),), jnp.float32)
    return dict(embeddings=embeddings, latent=latent, list_of=list_of, rank_of=rank_of, probes=probes)


RIDGE = 0.01

def chol_solve(gram, right_side):
    factor = jnp.linalg.cholesky(gram)
    order_n = gram.shape[0]
    forward = []
    for i in range(order_n):
        running = right_side[i]
        for j in range(i):
            running = running - factor[i, j] * forward[j]
        forward.append(running / factor[i, i])
    backward = [None] * order_n
    for i in reversed(range(order_n)):
        running = forward[i]
        for j in range(i + 1, order_n):
            running = running - factor[j, i] * backward[j]
        backward[i] = running / factor[i, i]
    return jnp.stack(backward)

def grams(left_blk, right_blk):
    return lax.dot_general(left_blk, right_blk, (((1,), (1,)), ((), ())), precision=lax.Precision.HIGHEST)

def plackett_luce(latent, list_of, rank_of):
    highest = jax.ops.segment_max(latent, list_of, num_segments=LISTS)
    shifted = jnp.exp(latent - highest[list_of])
    gradient = jnp.ones_like(latent)
    curvature = jnp.zeros_like(latent)
    for section_no in range(LIST_LEN):
        active = rank_of >= section_no
        totals = jax.ops.segment_sum(jnp.where(active, shifted, 0.0), list_of, num_segments=LISTS)
        chance = shifted / totals[list_of]
        gradient = gradient - jnp.where(active, chance, 0.0)
        curvature = curvature + jnp.where(active, chance * (1.0 - chance), 0.0)
    return (gradient, curvature)

def apply_kernel(scaled, embeddings):
    points = embeddings.astype(jnp.float32)
    sq_norm = lax.optimization_barrier(jnp.sum(points * points, axis=0))
    gamma = 2.0 / D
    block_len = min(1024, N)
    widened = scaled.astype(jnp.float32)

    def one_block(position):
        anchor = (position * block_len).astype(jnp.int32)
        part_pts = lax.dynamic_slice_in_dim(points, anchor, block_len, 1)
        part_sq = lax.dynamic_slice_in_dim(sq_norm, anchor, block_len, 0)
        inner_prod = jnp.dot(part_pts.T, points)
        kernel = jnp.exp(-gamma * (part_sq[:, None] + sq_norm[None, :] - 2.0 * inner_prod)).astype(jnp.bfloat16)
        kernel = lax.optimization_barrier(kernel).astype(jnp.float32)
        return jnp.dot(widened, kernel.T)
    blocks = lax.map(one_block, jnp.arange(N // block_len, dtype=jnp.int32))
    return jnp.transpose(blocks, (1, 0, 2)).reshape(SIDES, N)

def reference(embeddings, latent, list_of, rank_of, probes):
    gradient, curvature = plackett_luce(latent, list_of, rank_of)
    root_weight = jnp.sqrt(curvature + RIDGE)
    residual = jnp.concatenate([gradient[None, :], probes], axis=0)
    solution = jnp.zeros_like(residual)
    direction = residual
    res_gram = grams(residual, residual)
    for step_no in range(ITERS):
        scaled = (root_weight[None, :] * direction).astype(jnp.bfloat16)
        image = direction + root_weight[None, :] * apply_kernel(scaled, embeddings)
        dir_gram = grams(direction, image)
        step_coef = chol_solve(dir_gram, res_gram)
        solution = solution + jnp.dot(step_coef.T, direction, precision=lax.Precision.HIGHEST)
        residual = residual - jnp.dot(step_coef.T, image, precision=lax.Precision.HIGHEST)
        if step_no + 1 < ITERS:
            new_gram = grams(residual, residual)
            mix_coef = chol_solve(res_gram, new_gram)
            direction = residual + jnp.dot(mix_coef.T, direction, precision=lax.Precision.HIGHEST)
            res_gram = new_gram
    return (solution, residual)
```

```python
import jax
import jax.numpy as jnp
from jax import lax
from jax.experimental import pallas as pl
from jax.experimental.pallas import tpu as pltpu
from jax.sharding import Mesh
from jax.sharding import PartitionSpec as P

D = 64
SIDES = 16
LIST_LEN = 8
PT = 256
RIDGE = 0.01
GAMMA = 2.0 / D
ALL = ("y", "core", "z", "x")
GROUP_C = ("y", "x")
GROUP_R = ("core", "z")
GRP = 16
SET = GRP * PT
AUG = 80
R_STEP = 2
VMEM = 56 << 20

F32 = jnp.float32
BF16 = jnp.bfloat16


def hdot(a, b, dims):
    return lax.dot_general(
        a, b, (dims, ((), ())), precision=lax.Precision.HIGHEST, preferred_element_type=F32
    )


def split3(v):
    hi = v.astype(BF16).astype(F32)
    mid = (v - hi).astype(BF16).astype(F32)
    lo = (v - hi - mid).astype(BF16).astype(F32)
    return hi, mid, lo


def spd_solve(gram, right):
    n = gram.shape[0]
    lanes = lax.broadcasted_iota(jnp.int32, (n, n), 1)
    rows = lax.broadcasted_iota(jnp.int32, (n, n), 0)
    a, b = 0.5 * (gram + gram.T), right
    for k in range(n):
        pivot = a[k : k + 1, k : k + 1]
        column = a[:, k : k + 1]
        factor = jnp.where(rows[:, :1] == k, 0.0, column / pivot)
        a_row, b_row = a[k : k + 1, :], b[k : k + 1, :]
        a = a - factor * a_row
        b = b - factor * b_row
    diagonal = jnp.sum(jnp.where(lanes == rows, a, 0.0), axis=1, keepdims=True)
    return b / diagonal


def prepare(emb, latent, list_of, rank_of, probes, msg_c, msg_r, resid, weight):
    row = jnp.concatenate(
        [
            latent[...],
            list_of[...].astype(F32),
            rank_of[...].astype(F32),
            jnp.zeros((5, PT), F32),
        ],
        axis=0,
    )
    col = row.T
    same = col[:, 1:2] == row[1:2, :]
    highest = jnp.max(jnp.where(same, col[:, 0:1], -jnp.inf), axis=0, keepdims=True)
    shifted = jnp.exp(row[0:1, :] - highest)
    shifted_col = jnp.broadcast_to(shifted, (8, PT)).T[:, 0:1]
    gradient = jnp.ones((1, PT), F32)
    curvature = jnp.zeros((1, PT), F32)
    for k in range(LIST_LEN):
        held = jnp.where(col[:, 2:3] >= k, shifted_col, 0.0)
        totals = jnp.sum(jnp.where(same, held, 0.0), axis=0, keepdims=True)
        chance = shifted / totals
        active = row[2:3, :] >= k
        gradient = gradient - jnp.where(active, chance, 0.0)
        curvature = curvature + jnp.where(active, chance * (1.0 - chance), 0.0)
    w = jnp.sqrt(curvature + RIDGE)
    r0 = jnp.concatenate([gradient, probes[...]], axis=0)
    resid[...] = r0
    weight[...] = w
    points = emb[...].astype(F32)
    sq = -GAMMA * jnp.sum(points * points, axis=0, keepdims=True)
    parts = jnp.concatenate(split3(sq), axis=0)
    ones = jnp.ones((3, PT), F32)
    zeros = jnp.zeros((AUG - D - 6, PT), F32)
    to_c = jnp.concatenate([points, ones, parts, zeros, w * r0], axis=0).astype(BF16)
    to_r = jnp.concatenate([points * (2.0 * GAMMA), parts, ones, zeros], axis=0).astype(BF16)
    for g in range(GRP):
        msg_c[g] = to_c
        msg_r[g] = to_r


def first_apply(c_ref, r_ref, out, tile, left, vec):
    @pl.when(pl.program_id(0) == 0)
    def _():
        for g in range(GRP):
            left[g * PT : (g + 1) * PT, :] = c_ref[g, :AUG, :].T
            vec[:, g * PT : (g + 1) * PT] = c_ref[g, AUG:, :]

    right = jnp.concatenate([r_ref[i] for i in range(R_STEP)], axis=1)
    step = 512
    total = jnp.zeros((SIDES, R_STEP * PT), F32)
    for j in range(SET // step):
        at = slice(j * step, (j + 1) * step)
        exponent = jnp.dot(left[at, :], right, preferred_element_type=F32)
        kernel = jnp.exp(exponent).astype(BF16)
        tile[at, :] = kernel
        total += jnp.dot(vec[:, at], kernel, preferred_element_type=F32)
    for i in range(R_STEP):
        out[i] = total[:, i * PT : (i + 1) * PT]


def moments(all_ref, out):
    total = jnp.zeros((2 * SIDES, 2 * SIDES), F32)
    for g in range(GRP):
        block = all_ref[g, : 2 * SIDES, :]
        total += hdot(block, block, ((1,), (1,)))
    rr = total[:SIDES, :SIDES]
    ri = total[:SIDES, SIDES:]
    ii = total[SIDES:, SIDES:]
    packed = jnp.concatenate(
        [rr[:8], rr[8:], ri[:8], ri[8:], ii[:8], ii[8:], jnp.zeros((8, 32), F32)], axis=1
    )
    for g in range(GRP):
        out[g] = packed


def unpack(total, n):
    return jnp.concatenate(
        [total[:, 32 * n : 32 * n + 16], total[:, 32 * n + 16 : 32 * n + 32]], axis=0
    )


def second_apply(
    mom, all_ref, res_ref, img_ref, tile, out, sol1, res1, dir1, gram1, vec
):
    @pl.when(pl.program_id(0) == 0)
    def _():
        total = jnp.sum(mom[...], axis=0)
        rr, ri, ii = unpack(total, 0), unpack(total, 1), unpack(total, 2)
        step = spd_solve(ri, rr)
        cross = hdot(step, ri, ((0,), (1,)))
        new = rr - cross - cross.T + hdot(step, hdot(ii, step, ((1,), (0,))), ((0,), (0,)))
        mix = spd_solve(rr, new)
        gram1[...] = new

        def advance(r0, i0):
            r1 = r0 - hdot(step, i0, ((0,), (0,)))
            return r1, r1 + hdot(mix, r0, ((0,), (0,)))

        r1, d1 = advance(res_ref[...], img_ref[...])
        sol1[...] = hdot(step, res_ref[...], ((0,), (0,)))
        res1[...] = r1
        dir1[...] = d1
        for g in range(GRP):
            _, d1 = advance(all_ref[g, :SIDES, :], all_ref[g, SIDES : 2 * SIDES, :])
            w = all_ref[g, 2 * SIDES : 2 * SIDES + 1, :]
            vec[:, g * PT : (g + 1) * PT] = (w * d1).astype(BF16)

    total = jnp.dot(vec[...], tile[...], preferred_element_type=F32)
    for i in range(R_STEP):
        out[i] = total[:, i * PT : (i + 1) * PT]


def first_image(parts, base, w, out, image):
    total = parts[0]
    for g in range(1, GRP):
        total = total + parts[g]
    img = base[...] + w[...] * total
    image[...] = img
    message = jnp.concatenate([base[...], img, jnp.broadcast_to(w[...], (8, PT))], axis=0)
    for g in range(GRP):
        out[g] = message


def second_image(parts, base, w, out, image):
    total = parts[0]
    for g in range(1, GRP):
        total = total + parts[g]
    img = base[...] + w[...] * total
    image[...] = img
    gram = hdot(base[...], img, ((1,), (1,)))
    top = jnp.concatenate([gram[i : i + 1] for i in range(8)], axis=1)
    bottom = jnp.concatenate([gram[i : i + 1] for i in range(8, 16)], axis=1)
    packed = jnp.concatenate([top, bottom], axis=0)
    out[...] = jnp.broadcast_to(packed[None], out.shape)


def finish(grams, gram1, sol1, res1, dir1, img1, sol, res):
    total = jnp.sum(grams[...], axis=0)
    gram = jnp.concatenate(
        [total[i // 8 : i // 8 + 1, 16 * (i % 8) : 16 * (i % 8) + 16] for i in range(16)], axis=0
    )
    step = spd_solve(gram, gram1[...])
    sol[...] = sol1[...] + hdot(step, dir1[...], ((0,), (0,)))
    res[...] = res1[...] - hdot(step, img1[...], ((0,), (0,)))


def shape(*dims, dtype=F32):
    return jax.ShapeDtypeStruct(dims, dtype)


def call(body, out, **more):
    return pl.pallas_call(
        body,
        out_shape=out,
        compiler_params=pltpu.CompilerParams(vmem_limit_bytes=VMEM),
        **more,
    )


def whole(*dims):
    return pl.BlockSpec(dims, lambda i: (0,) * len(dims))


def per_device(embeddings, latent, list_of, rank_of, probes):
    msg_c, msg_r, res0, w = call(
        prepare,
        (
            shape(GRP, AUG + SIDES, PT, dtype=BF16),
            shape(GRP, AUG, PT, dtype=BF16),
            shape(SIDES, PT),
            shape(1, PT),
        ),
        name="prepare",
    )(embeddings, latent[None, :], list_of[None, :], rank_of[None, :], probes)
    all_c = lax.all_to_all(msg_c, GROUP_C, 0, 0, tiled=True)
    all_r = lax.all_to_all(msg_r, GROUP_R, 0, 0, tiled=True)

    n_steps = GRP // R_STEP
    part_spec = pl.BlockSpec((R_STEP, SIDES, PT), lambda i: (i, 0, 0))
    tile_spec = pl.BlockSpec((None, SET, R_STEP * PT), lambda i: (i, 0, 0))
    part, tiles = call(
        first_apply,
        (shape(GRP, SIDES, PT), shape(n_steps, SET, R_STEP * PT, dtype=BF16)),
        grid=(n_steps,),
        in_specs=[
            whole(GRP, AUG + SIDES, PT),
            pl.BlockSpec((R_STEP, AUG, PT), lambda i: (i, 0, 0)),
        ],
        out_specs=(part_spec, tile_spec),
        scratch_shapes=[pltpu.VMEM((SET, AUG), BF16), pltpu.VMEM((SIDES, SET), BF16)],
        name="first_apply",
    )(all_c, all_r)
    part = lax.all_to_all(part, GROUP_R, 0, 0, tiled=True)

    message, img0 = call(
        first_image, (shape(GRP, 2 * SIDES + 8, PT), shape(SIDES, PT)), name="first_image"
    )(part, res0, w)
    everyone = lax.all_to_all(message, GROUP_C, 0, 0, tiled=True)
    mom = call(moments, shape(GRP, 8, 128), name="moments")(everyone)
    mom = lax.all_to_all(mom, GROUP_R, 0, 0, tiled=True)

    part, sol1, res1, dir1, gram1 = call(
        second_apply,
        (
            shape(GRP, SIDES, PT),
            shape(SIDES, PT),
            shape(SIDES, PT),
            shape(SIDES, PT),
            shape(SIDES, SIDES),
        ),
        grid=(n_steps,),
        in_specs=[
            whole(GRP, 8, 128),
            whole(GRP, 2 * SIDES + 8, PT),
            whole(SIDES, PT),
            whole(SIDES, PT),
            tile_spec,
        ],
        out_specs=(
            part_spec,
            whole(SIDES, PT),
            whole(SIDES, PT),
            whole(SIDES, PT),
            whole(SIDES, SIDES),
        ),
        scratch_shapes=[pltpu.VMEM((SIDES, SET), BF16)],
        name="second_apply",
    )(mom, everyone, res0, img0, tiles)
    part = lax.all_to_all(part, GROUP_R, 0, 0, tiled=True)

    grams, img1 = call(
        second_image, (shape(256, 2, 128), shape(SIDES, PT)), name="second_image"
    )(part, dir1, w)
    grams = lax.all_to_all(grams, ALL, 0, 0, tiled=True)
    return call(finish, (shape(SIDES, PT), shape(SIDES, PT)), name="finish")(
        grams, gram1, sol1, res1, dir1, img1
    )


def solution(mesh):
    grid = Mesh(mesh.devices.reshape(4, 2, 8, 4), ALL)
    in_specs = (P(None, ALL), P(ALL), P(ALL), P(ALL), P(None, ALL))
    return jax.shard_map(
        per_device,
        mesh=grid,
        in_specs=in_specs,
        out_specs=(P(None, ALL), P(None, ALL)),
        check_vma=False,
    )
```

```python
import jax
import jax.numpy as jnp
from jax import lax
from jax.experimental import pallas as pl
from jax.experimental.pallas import tpu as pltpu
from jax.sharding import Mesh
from jax.sharding import PartitionSpec as P

D = 64
SIDES = 16
LIST_LEN = 8
PT = 256
RIDGE = 0.01
GAMMA = 2.0 / D
ALL = ("y", "core", "z", "x")
GROUP_C = ("y", "x")
GROUP_R = ("core", "z")
GRP = 16
DEPTH = 8
COLS = 2 * GRP * PT
ROWS = DEPTH * PT
AUG = 80
PIECES = 8
PIECE = COLS // PIECES

F32 = jnp.float32
BF16 = jnp.bfloat16


def hdot(a, b, dims):
    return lax.dot_general(
        a, b, (dims, ((), ())), precision=lax.Precision.HIGHEST, preferred_element_type=F32
    )


def split3(v):
    hi = v.astype(BF16).astype(F32)
    mid = (v - hi).astype(BF16).astype(F32)
    lo = (v - hi - mid).astype(BF16).astype(F32)
    return hi, mid, lo


def spd_solve(gram, right):
    n = gram.shape[0]
    lanes = lax.broadcasted_iota(jnp.int32, (n, n), 1)
    rows = lax.broadcasted_iota(jnp.int32, (n, n), 0)
    a, b = 0.5 * (gram + gram.T), right
    for k in range(n):
        pivot = a[k : k + 1, k : k + 1]
        column = a[:, k : k + 1]
        factor = jnp.where(rows[:, :1] == k, 0.0, column / pivot)
        a_row, b_row = a[k : k + 1, :], b[k : k + 1, :]
        a = a - factor * a_row
        b = b - factor * b_row
    diagonal = jnp.sum(jnp.where(lanes == rows, a, 0.0), axis=1, keepdims=True)
    return b / diagonal


def prepare(emb, latent, list_of, rank_of, probes, msg_c, msg_r, resid, weight):
    row = jnp.concatenate(
        [
            latent[...],
            list_of[...].astype(F32),
            rank_of[...].astype(F32),
            jnp.zeros((5, PT), F32),
        ],
        axis=0,
    )
    col = row.T
    same = col[:, 1:2] == row[1:2, :]
    highest = jnp.max(jnp.where(same, col[:, 0:1], -jnp.inf), axis=0, keepdims=True)
    shifted = jnp.exp(row[0:1, :] - highest)
    shifted_col = jnp.broadcast_to(shifted, (8, PT)).T[:, 0:1]
    gradient = jnp.ones((1, PT), F32)
    curvature = jnp.zeros((1, PT), F32)
    for k in range(LIST_LEN):
        held = jnp.where(col[:, 2:3] >= k, shifted_col, 0.0)
        totals = jnp.sum(jnp.where(same, held, 0.0), axis=0, keepdims=True)
        chance = shifted / totals
        active = row[2:3, :] >= k
        gradient = gradient - jnp.where(active, chance, 0.0)
        curvature = curvature + jnp.where(active, chance * (1.0 - chance), 0.0)
    w = jnp.sqrt(curvature + RIDGE)
    r0 = jnp.concatenate([gradient, probes[...]], axis=0)
    resid[...] = r0
    weight[...] = w
    scaled = w * r0
    high = scaled.astype(BF16)
    low = (scaled - high.astype(F32)).astype(BF16)
    for g in range(GRP):
        msg_c[g, :D, :] = emb[...]
        msg_c[g, D : D + SIDES, :] = high
        msg_c[g, D + SIDES :, :] = low
    for g in range(DEPTH):
        msg_r[g] = emb[...]


def norm_rows(points):
    sq = -GAMMA * jnp.sum(points * points, axis=0, keepdims=True)
    return jnp.concatenate(split3(sq), axis=0)


def first_apply(own, other, r_ref, out, *more):
    tile, (left, vec) = more[:PIECES], more[PIECES:]
    ones = jnp.ones((3, PT), F32)
    zeros = jnp.zeros((AUG - D - 6, PT), F32)
    for half, ref in enumerate((own, other)):
        for g in range(GRP):
            at = slice((half * GRP + g) * PT, (half * GRP + g + 1) * PT)
            points = ref[g, :D, :].astype(F32)
            rows = jnp.concatenate([points, ones, norm_rows(points), zeros], axis=0)
            left[at, :] = rows.astype(BF16).T
            vec[:, at] = ref[g, D : D + SIDES, :]
    columns = []
    for g in range(DEPTH):
        points = r_ref[g].astype(F32)
        rows = [points * (2.0 * GAMMA), norm_rows(points), ones, zeros]
        columns.append(jnp.concatenate(rows, axis=0).astype(BF16))
    right = jnp.concatenate(columns, axis=1)
    step = 256
    total = jnp.zeros((SIDES, ROWS), F32)
    for j in range(COLS // step):
        at = slice(j * step, (j + 1) * step)
        exponent = jnp.dot(left[at, :], right, preferred_element_type=F32)
        kernel = jnp.exp(exponent).astype(BF16)
        tile[j * step // PIECE][pl.ds(j * step % PIECE, step), :] = kernel
        total += jnp.dot(vec[:, at], kernel, preferred_element_type=F32)
    for g in range(DEPTH):
        out[g] = total[:, g * PT : (g + 1) * PT]


def unpack(total, n):
    return jnp.concatenate(
        [total[:, 32 * n : 32 * n + 16], total[:, 32 * n + 16 : 32 * n + 32]], axis=0
    )


def first_image(parts, base, w, out, image):
    total = parts[0]
    for g in range(1, DEPTH):
        total = total + parts[g]
    r0 = base[...]
    i0 = r0 + w[...] * total
    image[...] = i0
    both = jnp.concatenate([r0, i0], axis=0)
    gram = hdot(both, both, ((1,), (1,)))
    rr, ri, ii = gram[:SIDES, :SIDES], gram[:SIDES, SIDES:], gram[SIDES:, SIDES:]
    packed = [rr[:8], rr[8:], ri[:8], ri[8:], ii[:8], ii[8:], jnp.zeros((8, 160), F32)]
    message = jnp.concatenate([w[...] * i0, jnp.concatenate(packed, axis=1)], axis=0)
    for g in range(GRP):
        out[g] = message


def gram_sum(own, out):
    total = own[0]
    for g in range(1, GRP):
        total = total + own[g]
    for g in range(GRP):
        out[g] = total


def second_apply(
    mom, own_i, other_i, own_s, other_s, res_ref, img_ref, *more
):
    tile, (out, sol1, res1, dir1, gram1) = more[:PIECES], more[PIECES:]
    total = jnp.sum(mom[...], axis=0)
    rr, ri, ii = unpack(total, 0), unpack(total, 1), unpack(total, 2)
    step = spd_solve(ri, rr)
    cross = hdot(step, ri, ((0,), (1,)))
    new = rr - cross - cross.T + hdot(step, hdot(ii, step, ((1,), (0,))), ((0,), (0,)))
    mix = spd_solve(rr, new)
    gram1[...] = new
    r0, i0 = res_ref[...], img_ref[...]
    sol1[...] = hdot(step, r0, ((0,), (0,)))
    r1 = r0 - hdot(step, i0, ((0,), (0,)))
    res1[...] = r1
    dir1[...] = r1 + hdot(mix, r0, ((0,), (0,)))
    rows = lax.broadcasted_iota(jnp.int32, (SIDES, SIDES), 0)
    lanes = lax.broadcasted_iota(jnp.int32, (SIDES, SIDES), 1)
    coef = jnp.concatenate([jnp.where(rows == lanes, 1.0, 0.0) + mix, -step], axis=0)
    vec = []
    for i_ref, s_ref in ((own_i, own_s), (other_i, other_s)):
        for g in range(GRP):
            wr = s_ref[g, :SIDES, :].astype(F32) + s_ref[g, SIDES:, :].astype(F32)
            both = jnp.concatenate([wr, i_ref[g]], axis=0)
            vec.append(hdot(coef, both, ((0,), (0,))).astype(BF16))
    total = jnp.zeros((SIDES, ROWS), F32)
    for j in range(len(vec)):
        kernel = tile[j * PT // PIECE][pl.ds(j * PT % PIECE, PT), :]
        total += jnp.dot(vec[j], kernel, preferred_element_type=F32)
    for g in range(DEPTH):
        out[g] = total[:, g * PT : (g + 1) * PT]


def second_image(parts, base, w, out, image):
    total = parts[0]
    for g in range(1, DEPTH):
        total = total + parts[g]
    img = base[...] + w[...] * total
    image[...] = img
    gram = hdot(base[...], img, ((1,), (1,)))
    top = jnp.concatenate([gram[i : i + 1] for i in range(8)], axis=1)
    bottom = jnp.concatenate([gram[i : i + 1] for i in range(8, 16)], axis=1)
    packed = jnp.concatenate([top, bottom], axis=0)
    out[...] = jnp.broadcast_to(packed[None], out.shape)


def finish(grams, gram1, sol1, res1, dir1, img1, sol, res):
    total = jnp.sum(grams[...], axis=0)
    gram = jnp.concatenate(
        [total[i // 8 : i // 8 + 1, 16 * (i % 8) : 16 * (i % 8) + 16] for i in range(16)], axis=0
    )
    step = spd_solve(gram, gram1[...])
    sol[...] = sol1[...] + hdot(step, dir1[...], ((0,), (0,)))
    res[...] = res1[...] - hdot(step, img1[...], ((0,), (0,)))


def shape(*dims, dtype=F32):
    return jax.ShapeDtypeStruct(dims, dtype)


def call(body, out, vmem=8, **more):
    return pl.pallas_call(
        body,
        out_shape=out,
        compiler_params=pltpu.CompilerParams(vmem_limit_bytes=vmem << 20),
        **more,
    )


def block(*dims, at=None):
    return pl.BlockSpec(dims, lambda i: at or (0,) * len(dims))


def swap_cores(array):
    return lax.ppermute(array, "core", ((0, 1), (1, 0)))


def per_device(embeddings, latent, list_of, rank_of, probes):
    resident = pl.BlockSpec(memory_space=pltpu.VMEM)
    msg_c, msg_r, res0, w = call(
        prepare,
        (
            shape(GRP, D + 2 * SIDES, PT, dtype=BF16),
            shape(DEPTH, D, PT, dtype=BF16),
            shape(SIDES, PT),
            shape(1, PT),
        ),
        name="prepare",
    )(embeddings, latent[None, :], list_of[None, :], rank_of[None, :], probes)
    own_c = lax.all_to_all(msg_c, GROUP_C, 0, 0, tiled=True)
    other_c = swap_cores(own_c)
    all_r = lax.all_to_all(msg_r, "z", 0, 0, tiled=True)

    part, *tile = call(
        first_apply,
        (shape(DEPTH, SIDES, PT), *([pltpu.VMEM((PIECE, ROWS), BF16)] * PIECES)),
        vmem=16,
        out_specs=(pl.BlockSpec((DEPTH, SIDES, PT), lambda: (0, 0, 0)), *([resident] * PIECES)),
        scratch_shapes=[pltpu.VMEM((COLS, AUG), BF16), pltpu.VMEM((SIDES, COLS), BF16)],
        name="first_apply",
    )(own_c, other_c, all_r)
    part = lax.all_to_all(part, "z", 0, 0, tiled=True)

    message, img0 = call(
        first_image, (shape(GRP, SIDES + 8, PT), shape(SIDES, PT)), name="first_image"
    )(part, res0, w)
    own_i = lax.all_to_all(message, GROUP_C, 0, 0, tiled=True)
    other_i = swap_cores(own_i)
    mom = call(
        gram_sum,
        shape(GRP, 8, 128),
        grid=(1,),
        in_specs=[block(GRP, 8, 128, at=(0, 2, 0))],
        out_specs=block(GRP, 8, 128),
        name="gram_sum",
    )(own_i)
    mom = lax.all_to_all(mom, GROUP_R, 0, 0, tiled=True)

    images = block(GRP, SIDES, PT)
    scaled = block(GRP, 2 * SIDES, PT, at=(0, 2, 0))
    own = block(SIDES, PT)
    part, sol1, res1, dir1, gram1 = call(
        second_apply,
        (
            shape(DEPTH, SIDES, PT),
            shape(SIDES, PT),
            shape(SIDES, PT),
            shape(SIDES, PT),
            shape(SIDES, SIDES),
        ),
        vmem=12,
        grid=(1,),
        in_specs=[block(GRP, 8, 128), images, images, scaled, scaled, own, own] + [resident] * PIECES,
        out_specs=(block(DEPTH, SIDES, PT), own, own, own, block(SIDES, SIDES)),
        name="second_apply",
    )(mom, own_i, other_i, own_c, other_c, res0, img0, *tile)
    part = lax.all_to_all(part, "z", 0, 0, tiled=True)

    grams, img1 = call(
        second_image, (shape(256, 2, 128), shape(SIDES, PT)), name="second_image"
    )(part, dir1, w)
    grams = lax.all_to_all(grams, ALL, 0, 0, tiled=True)
    return call(finish, (shape(SIDES, PT), shape(SIDES, PT)), name="finish")(
        grams, gram1, sol1, res1, dir1, img1
    )


def solution(mesh):
    grid = Mesh(mesh.devices.reshape(4, 2, 8, 4), ALL)
    in_specs = (P(None, ALL), P(ALL), P(ALL), P(ALL), P(None, ALL))
    return jax.shard_map(
        per_device,
        mesh=grid,
        in_specs=in_specs,
        out_specs=(P(None, ALL), P(None, ALL)),
        check_vma=False,
    )
```

```python
import jax
import jax.numpy as jnp
from jax import lax
from jax.experimental import pallas as pl
from jax.experimental.pallas import tpu as pltpu
from jax.sharding import Mesh
from jax.sharding import PartitionSpec as P

D = 64
SIDES = 16
LIST_LEN = 8
PT = 256
RIDGE = 0.01
GAMMA = 2.0 / D
ALL = ("y", "core", "z", "x")
GROUP_C = ("y", "x")
GROUP_R = ("core", "z")
GRP = 16
DEPTH = 8
PAIRS = DEPTH // 2
HALF = GRP * PT
COLS = 2 * HALF
ROWS = DEPTH * PT
AUG = 80
VMEM_ALL = 60
PIECES = 16
PIECE = COLS // PIECES

F32 = jnp.float32
BF16 = jnp.bfloat16


def hdot(a, b, dims):
    return lax.dot_general(
        a, b, (dims, ((), ())), precision=lax.Precision.HIGHEST, preferred_element_type=F32
    )


def split3(v):
    hi = v.astype(BF16).astype(F32)
    mid = (v - hi).astype(BF16).astype(F32)
    lo = (v - hi - mid).astype(BF16).astype(F32)
    return hi, mid, lo


def spd_solve(gram, right):
    n = gram.shape[0]
    lanes = lax.broadcasted_iota(jnp.int32, (n, n), 1)
    rows = lax.broadcasted_iota(jnp.int32, (n, n), 0)
    a, b = 0.5 * (gram + gram.T), right
    for k in range(n):
        pivot = a[k : k + 1, k : k + 1]
        column = a[:, k : k + 1]
        factor = jnp.where(rows[:, :1] == k, 0.0, column / pivot)
        a_row, b_row = a[k : k + 1, :], b[k : k + 1, :]
        a = a - factor * a_row
        b = b - factor * b_row
    diagonal = jnp.sum(jnp.where(lanes == rows, a, 0.0), axis=1, keepdims=True)
    return b / diagonal


def prepare(
    emb_in, latent_in, list_in, rank_in, probes_in,
    msg_c, emb, resid, weight,
    latent, list_of, rank_of, probes, sems,
):
    pairs = (
        (latent_in, latent), (list_in, list_of), (rank_in, rank_of), (probes_in, probes), (emb_in, emb),
    )
    copies = [pltpu.make_async_copy(a, b, sems.at[i]) for i, (a, b) in enumerate(pairs)]
    for copy in copies:
        copy.start()
    for copy in copies[:3]:
        copy.wait()
    row = jnp.concatenate(
        [
            latent[...],
            list_of[...].astype(F32),
            rank_of[...].astype(F32),
            jnp.zeros((5, PT), F32),
        ],
        axis=0,
    )
    col = row.T
    same = col[:, 1:2] == row[1:2, :]
    highest = jnp.max(jnp.where(same, col[:, 0:1], -jnp.inf), axis=0, keepdims=True)
    shifted = jnp.exp(row[0:1, :] - highest)
    shifted_col = jnp.broadcast_to(shifted, (8, PT)).T[:, 0:1]
    gradient = jnp.ones((1, PT), F32)
    curvature = jnp.zeros((1, PT), F32)
    for k in range(LIST_LEN):
        held = jnp.where(col[:, 2:3] >= k, shifted_col, 0.0)
        totals = jnp.sum(jnp.where(same, held, 0.0), axis=0, keepdims=True)
        chance = shifted / totals
        active = row[2:3, :] >= k
        gradient = gradient - jnp.where(active, chance, 0.0)
        curvature = curvature + jnp.where(active, chance * (1.0 - chance), 0.0)
    w = jnp.sqrt(curvature + RIDGE)
    copies[3].wait()
    copies[4].wait()
    r0 = jnp.concatenate([gradient, probes[...]], axis=0)
    resid[...] = r0
    weight[...] = w
    scaled = w * r0
    high = scaled.astype(BF16)
    low = (scaled - high.astype(F32)).astype(BF16)
    for g in range(GRP):
        msg_c[g, :D, :] = emb[...]
        msg_c[g, D : D + SIDES, :] = high
        msg_c[g, D + SIDES :, :] = low


def norm_rows(points):
    sq = -GAMMA * jnp.sum(points * points, axis=0, keepdims=True)
    return jnp.concatenate(split3(sq), axis=0)


def half_apply(c_ref, right, tile, left, vec):
    ones = jnp.ones((3, PT), F32)
    zeros = jnp.zeros((AUG - D - 6, PT), F32)
    for g in range(GRP):
        at = slice(g * PT, (g + 1) * PT)
        points = c_ref[g, :D, :].astype(F32)
        rows = jnp.concatenate([points, ones, norm_rows(points), zeros], axis=0)
        left[at, :] = rows.astype(BF16).T
        vec[:, at] = c_ref[g, D : D + SIDES, :]
    step = 256
    total = jnp.zeros((SIDES, ROWS), F32)
    for j in range(HALF // step):
        at = slice(j * step, (j + 1) * step)
        exponent = jnp.dot(left[at, :], right[...], preferred_element_type=F32)
        kernel = jnp.exp(exponent).astype(BF16)
        tile[j * step // PIECE][pl.ds(j * step % PIECE, step), :] = kernel
        total += jnp.dot(vec[:, at], kernel, preferred_element_type=F32)
    return total


def place_blocks(place, out, total):
    for k in range(DEPTH):
        out[lax.bitwise_xor(place[0], k)] = total[:, k * PT : (k + 1) * PT]


def first_half(c_ref, *more):
    r_refs, out, right, more = more[:PAIRS], more[PAIRS], more[PAIRS + 1], more[PAIRS + 2 :]
    ones = jnp.ones((3, PT), F32)
    zeros = jnp.zeros((AUG - D - 6, PT), F32)
    for k in range(DEPTH):
        points = r_refs[k // 2][:, k % 2 * PT : (k % 2 + 1) * PT].astype(F32)
        rows = [points * (2.0 * GAMMA), norm_rows(points), ones, zeros]
        right[:, k * PT : (k + 1) * PT] = jnp.concatenate(rows, axis=0).astype(BF16)
    out[...] = half_apply(c_ref, right, more[: PIECES // 2], *more[PIECES // 2 :])


def second_half(place, c_ref, right, before, out, *more):
    total = half_apply(c_ref, right, more[: PIECES // 2], *more[PIECES // 2 :])
    place_blocks(place, out, total + before[...])


def unpack(total, n):
    return jnp.concatenate(
        [total[:, 32 * n : 32 * n + 16], total[:, 32 * n + 16 : 32 * n + 32]], axis=0
    )


def first_image(parts, base, w, out, image):
    total = parts[0]
    for g in range(1, DEPTH):
        total = total + parts[g]
    r0 = base[...]
    i0 = r0 + w[...] * total
    image[...] = i0
    both = jnp.concatenate([r0, i0], axis=0)
    gram = hdot(both, both, ((1,), (1,)))
    rr, ri, ii = gram[:SIDES, :SIDES], gram[:SIDES, SIDES:], gram[SIDES:, SIDES:]
    packed = [rr[:8], rr[8:], ri[:8], ri[8:], ii[:8], ii[8:], jnp.zeros((8, 160), F32)]
    message = jnp.concatenate([w[...] * i0, jnp.concatenate(packed, axis=1)], axis=0)
    for g in range(GRP):
        out[g] = message


def gram_sum(own, out):
    total = own[0]
    for g in range(1, GRP):
        total = total + own[g]
    for g in range(GRP):
        out[g] = total


def second_apply(
    place, mom, own_i, other_i, own_s, other_s, res_ref, img_ref, *more
):
    tile, (out, sol1, res1, dir1, gram1) = more[:PIECES], more[PIECES:]
    total = jnp.sum(mom[...], axis=0)
    rr, ri, ii = unpack(total, 0), unpack(total, 1), unpack(total, 2)
    step = spd_solve(ri, rr)
    cross = hdot(step, ri, ((0,), (1,)))
    new = rr - cross - cross.T + hdot(step, hdot(ii, step, ((1,), (0,))), ((0,), (0,)))
    mix = spd_solve(rr, new)
    gram1[...] = new
    r0, i0 = res_ref[...], img_ref[...]
    sol1[...] = hdot(step, r0, ((0,), (0,)))
    r1 = r0 - hdot(step, i0, ((0,), (0,)))
    res1[...] = r1
    dir1[...] = r1 + hdot(mix, r0, ((0,), (0,)))
    rows = lax.broadcasted_iota(jnp.int32, (SIDES, SIDES), 0)
    lanes = lax.broadcasted_iota(jnp.int32, (SIDES, SIDES), 1)
    coef = jnp.concatenate([jnp.where(rows == lanes, 1.0, 0.0) + mix, -step], axis=0)
    vec = []
    for i_ref, s_ref in ((own_i, own_s), (other_i, other_s)):
        for g in range(GRP):
            wr = s_ref[g, :SIDES, :].astype(F32) + s_ref[g, SIDES:, :].astype(F32)
            both = jnp.concatenate([wr, i_ref[g]], axis=0)
            vec.append(hdot(coef, both, ((0,), (0,))).astype(BF16))
    total = jnp.zeros((SIDES, ROWS), F32)
    for j in range(len(vec)):
        kernel = tile[j * PT // PIECE][pl.ds(j * PT % PIECE, PT), :]
        total += jnp.dot(vec[j], kernel, preferred_element_type=F32)
    place_blocks(place, out, total)


def second_image(parts, base, w, out, image):
    total = parts[0]
    for g in range(1, DEPTH):
        total = total + parts[g]
    img = base[...] + w[...] * total
    image[...] = img
    gram = hdot(base[...], img, ((1,), (1,)))
    gram = 0.5 * (gram + gram.T)
    high = gram.astype(BF16).astype(F32)
    rows = lax.broadcasted_iota(jnp.int32, (SIDES, SIDES), 0)
    lanes = lax.broadcasted_iota(jnp.int32, (SIDES, SIDES), 1)
    gram = jnp.where(rows <= lanes, high, gram - high)
    top = jnp.concatenate([gram[i : i + 1] for i in range(8)], axis=1)
    bottom = jnp.concatenate([gram[i : i + 1] for i in range(8, 16)], axis=1)
    packed = jnp.concatenate([top, bottom], axis=0).astype(BF16)
    out[...] = jnp.broadcast_to(packed[None], out.shape)


def finish(grams, gram1, sol1, res1, dir1, img1, sol, res):
    total = jnp.sum(grams[...].astype(F32), axis=0)
    gram = jnp.concatenate(
        [total[i // 8 : i // 8 + 1, 16 * (i % 8) : 16 * (i % 8) + 16] for i in range(16)], axis=0
    )
    rows = lax.broadcasted_iota(jnp.int32, (SIDES, SIDES), 0)
    lanes = lax.broadcasted_iota(jnp.int32, (SIDES, SIDES), 1)
    gram = gram + jnp.where(rows == lanes, 0.0, gram.T)
    step = spd_solve(gram, gram1[...])
    sol[...] = sol1[...] + hdot(step, dir1[...], ((0,), (0,)))
    res[...] = res1[...] - hdot(step, img1[...], ((0,), (0,)))


def shape(*dims, dtype=F32):
    return jax.ShapeDtypeStruct(dims, dtype)


def call(body, out, vmem=8, **more):
    return pl.pallas_call(
        body,
        out_shape=out,
        compiler_params=pltpu.CompilerParams(vmem_limit_bytes=int(vmem * 2**20)),
        **more,
    )


def block(*dims, at=None):
    return pl.BlockSpec(dims, lambda i: at or (0,) * len(dims))


def swap_along_z(array, k):
    return lax.ppermute(array, "z", [(i, i ^ k) for i in range(DEPTH)])


def swap_cores(array):
    return lax.ppermute(array, "core", ((0, 1), (1, 0)))


def per_device(embeddings, latent, list_of, rank_of, probes):
    resident = pl.BlockSpec(memory_space=pltpu.VMEM)
    anywhere = pl.BlockSpec(memory_space=pl.ANY)
    msg_c, points, res0, w = call(
        prepare,
        (
            shape(GRP, D + 2 * SIDES, PT, dtype=BF16),
            shape(D, PT, dtype=BF16),
            shape(SIDES, PT),
            shape(1, PT),
        ),
        vmem=VMEM_ALL,
        in_specs=[anywhere] * 5,
        scratch_shapes=[
            pltpu.VMEM((1, PT), F32),
            pltpu.VMEM((1, PT), jnp.int32),
            pltpu.VMEM((1, PT), jnp.int32),
            pltpu.VMEM((SIDES - 1, PT), F32),
            pltpu.SemaphoreType.DMA((5,)),
        ],
        name="prepare",
    )(embeddings, latent[None, :], list_of[None, :], rank_of[None, :], probes)
    own_c = lax.all_to_all(msg_c, GROUP_C, 0, 0, tiled=True)
    pair = jnp.concatenate([points, swap_along_z(points, 1)], axis=1)
    all_r = [pair] + [swap_along_z(pair, k) for k in range(2, DEPTH, 2)]
    own_c, all_r = lax.optimization_barrier((own_c, all_r))
    other_c = swap_cores(own_c)

    place = lax.axis_index("z").astype(jnp.int32)[None]
    half_tile = [pltpu.VMEM((PIECE, ROWS), BF16)] * (PIECES // 2)
    scratch = [pltpu.VMEM((HALF, AUG), BF16), pltpu.VMEM((SIDES, HALF), BF16)]
    in_vmem = pl.BlockSpec(memory_space=pltpu.VMEM)
    in_smem = pl.BlockSpec(memory_space=pltpu.SMEM)
    part, right, *tile = call(
        first_half,
        (shape(SIDES, ROWS), shape(AUG, ROWS, dtype=BF16), *half_tile),
        in_specs=[in_vmem] * (1 + PAIRS),
        out_specs=[in_vmem] * (2 + PIECES // 2),
        scratch_shapes=scratch,
        name="first_half",
    )(own_c, *all_r)
    part, *more = call(
        second_half,
        (shape(DEPTH, SIDES, PT), *half_tile),
        in_specs=[in_smem] + [in_vmem] * 3,
        out_specs=[in_vmem] * (1 + PIECES // 2),
        scratch_shapes=scratch,
        name="second_half",
    )(place, other_c, right, part)
    tile = tile + more
    part = lax.all_to_all(part, "z", 0, 0, tiled=True)

    message, img0 = call(
        first_image, (shape(GRP, SIDES + 8, PT), shape(SIDES, PT)), name="first_image"
    )(part, res0, w)
    own_i = lax.all_to_all(message, GROUP_C, 0, 0, tiled=True)
    other_i = swap_cores(own_i)
    mom = call(
        gram_sum,
        shape(GRP, 8, 128),
        grid=(1,),
        in_specs=[block(GRP, 8, 128, at=(0, 2, 0))],
        out_specs=block(GRP, 8, 128),
        name="gram_sum",
    )(own_i)
    mom = lax.all_to_all(mom, GROUP_R, 0, 0, tiled=True)

    images = block(GRP, SIDES, PT)
    scaled = block(GRP, 2 * SIDES, PT, at=(0, 2, 0))
    own = block(SIDES, PT)
    part, sol1, res1, dir1, gram1 = call(
        second_apply,
        (
            shape(DEPTH, SIDES, PT),
            shape(SIDES, PT),
            shape(SIDES, PT),
            shape(SIDES, PT),
            shape(SIDES, SIDES),
        ),
        grid=(1,),
        in_specs=[in_smem, block(GRP, 8, 128), images, images, scaled, scaled, own, own] + [resident] * PIECES,
        out_specs=(block(DEPTH, SIDES, PT), own, own, own, block(SIDES, SIDES)),
        name="second_apply",
    )(place, mom, own_i, other_i, own_c, other_c, res0, img0, *tile)
    part = lax.all_to_all(part, "z", 0, 0, tiled=True)

    grams, img1 = call(
        second_image, (shape(256, 2, 128, dtype=BF16), shape(SIDES, PT)), name="second_image"
    )(part, dir1, w)
    grams = lax.all_to_all(grams, ALL, 0, 0, tiled=True)
    return call(finish, (shape(SIDES, PT), shape(SIDES, PT)), name="finish")(
        grams, gram1, sol1, res1, dir1, img1
    )


def solution(mesh):
    grid = Mesh(mesh.devices.reshape(4, 2, 8, 4), ALL)
    in_specs = (P(None, ALL), P(ALL), P(ALL), P(ALL), P(None, ALL))
    return jax.shard_map(
        per_device,
        mesh=grid,
        in_specs=in_specs,
        out_specs=(P(None, ALL), P(None, ALL)),
        check_vma=False,
    )
```

```python
import jax
import jax.numpy as jnp
from jax import lax
from jax.experimental import pallas as pl
from jax.experimental.pallas import tpu as pltpu
from jax.sharding import Mesh
from jax.sharding import PartitionSpec as P

D = 64
SIDES = 16
LIST_LEN = 8
PT = 256
RIDGE = 0.01
GAMMA = 2.0 / D
ALL = ("y", "core", "z", "x")
GROUP_C = ("y", "x")
GROUP_R = ("core", "z")
GRP = 16
DEPTH = 8
PAIRS = DEPTH // 2
HALF = GRP * PT
COLS = 2 * HALF
ROWS = DEPTH * PT
AUG = 80
VMEM_ALL = 60
PIECES = 16
PIECE = COLS // PIECES

F32 = jnp.float32
BF16 = jnp.bfloat16


def hdot(a, b, dims):
    return lax.dot_general(
        a, b, (dims, ((), ())), precision=lax.Precision.HIGHEST, preferred_element_type=F32
    )


def split3(v):
    hi = v.astype(BF16).astype(F32)
    mid = (v - hi).astype(BF16).astype(F32)
    lo = (v - hi - mid).astype(BF16).astype(F32)
    return hi, mid, lo


def spd_solve(gram, right):
    n = gram.shape[0]
    rows = lax.broadcasted_iota(jnp.int32, right.shape, 0)
    gram = 0.5 * (gram + gram.T)
    columns = [jnp.broadcast_to(gram[:, k : k + 1], right.shape) for k in range(n)]
    diagonal = jnp.ones(right.shape, F32)
    for k in range(n):
        pivot = columns[k][k : k + 1, :]
        scale = 1.0 / pivot
        factor = jnp.where(rows == k, 0.0, columns[k])
        diagonal = jnp.where(rows == k, scale, diagonal)
        for j in range(k + 1, n):
            columns[j] = columns[j] - factor * (columns[j][k : k + 1, :] * scale)
        right = right - factor * (right[k : k + 1, :] * scale)
    return right * diagonal


def prepare(
    emb_in, latent_in, list_in, rank_in, probes_in,
    msg_c, emb, resid, weight,
    latent, list_of, rank_of, probes, sems,
):
    pairs = (
        (latent_in, latent), (list_in, list_of), (rank_in, rank_of), (probes_in, probes), (emb_in, emb),
    )
    copies = [pltpu.make_async_copy(a, b, sems.at[i]) for i, (a, b) in enumerate(pairs)]
    for copy in copies:
        copy.start()
    for copy in copies[:3]:
        copy.wait()
    row = jnp.concatenate(
        [
            latent[...],
            list_of[...].astype(F32),
            rank_of[...].astype(F32),
            jnp.zeros((5, PT), F32),
        ],
        axis=0,
    )
    col = row.T
    same = col[:, 1:2] == row[1:2, :]
    highest = jnp.max(jnp.where(same, col[:, 0:1], -jnp.inf), axis=0, keepdims=True)
    shifted = jnp.exp(row[0:1, :] - highest)
    shifted_col = jnp.broadcast_to(shifted, (8, PT)).T[:, 0:1]
    gradient = jnp.ones((1, PT), F32)
    curvature = jnp.zeros((1, PT), F32)
    for k in range(LIST_LEN):
        held = jnp.where(col[:, 2:3] >= k, shifted_col, 0.0)
        totals = jnp.sum(jnp.where(same, held, 0.0), axis=0, keepdims=True)
        chance = shifted / totals
        active = row[2:3, :] >= k
        gradient = gradient - jnp.where(active, chance, 0.0)
        curvature = curvature + jnp.where(active, chance * (1.0 - chance), 0.0)
    w = jnp.sqrt(curvature + RIDGE)
    copies[3].wait()
    copies[4].wait()
    r0 = jnp.concatenate([gradient, probes[...]], axis=0)
    resid[...] = r0
    weight[...] = w
    scaled = w * r0
    high = scaled.astype(BF16)
    low = (scaled - high.astype(F32)).astype(BF16)
    for g in range(GRP):
        msg_c[g, :D, :] = emb[...]
        msg_c[g, D : D + SIDES, :] = high
        msg_c[g, D + SIDES :, :] = low


def norm_rows(points):
    sq = -GAMMA * jnp.sum(points * points, axis=0, keepdims=True)
    return jnp.concatenate(split3(sq), axis=0)


def half_apply(c_ref, right, tile, left, vec):
    ones = jnp.ones((3, PT), F32)
    zeros = jnp.zeros((AUG - D - 6, PT), F32)
    for g in range(GRP):
        at = slice(g * PT, (g + 1) * PT)
        points = c_ref[g, :D, :].astype(F32)
        rows = jnp.concatenate([points, ones, norm_rows(points), zeros], axis=0)
        left[at, :] = rows.astype(BF16).T
        vec[:, at] = c_ref[g, D : D + SIDES, :]
    step = 256
    total = jnp.zeros((SIDES, ROWS), F32)
    for j in range(HALF // step):
        at = slice(j * step, (j + 1) * step)
        exponent = jnp.dot(left[at, :], right[...], preferred_element_type=F32)
        kernel = jnp.exp(exponent).astype(BF16)
        tile[j * step // PIECE][pl.ds(j * step % PIECE, step), :] = kernel
        total += jnp.dot(vec[:, at], kernel, preferred_element_type=F32)
    return total


def place_blocks(place, out, total):
    for k in range(DEPTH):
        out[lax.bitwise_xor(place[0], k)] = total[:, k * PT : (k + 1) * PT]


def first_half(c_ref, *more):
    r_refs, out, right, more = more[:PAIRS], more[PAIRS], more[PAIRS + 1], more[PAIRS + 2 :]
    ones = jnp.ones((3, PT), F32)
    zeros = jnp.zeros((AUG - D - 6, PT), F32)
    for k in range(DEPTH):
        points = r_refs[k // 2][:, k % 2 * PT : (k % 2 + 1) * PT].astype(F32)
        rows = [points * (2.0 * GAMMA), norm_rows(points), ones, zeros]
        right[:, k * PT : (k + 1) * PT] = jnp.concatenate(rows, axis=0).astype(BF16)
    out[...] = half_apply(c_ref, right, more[: PIECES // 2], *more[PIECES // 2 :])


def second_half(place, c_ref, right, before, out, *more):
    total = half_apply(c_ref, right, more[: PIECES // 2], *more[PIECES // 2 :])
    place_blocks(place, out, total + before[...])


def unpack(total, n):
    return jnp.concatenate(
        [total[:, 32 * n : 32 * n + 16], total[:, 32 * n + 16 : 32 * n + 32]], axis=0
    )


def first_image(parts, base, w, out, image):
    total = parts[0]
    for g in range(1, DEPTH):
        total = total + parts[g]
    r0 = base[...]
    i0 = r0 + w[...] * total
    image[...] = i0
    both = jnp.concatenate([r0, i0], axis=0)
    gram = hdot(both, both, ((1,), (1,)))
    rr, ri, ii = gram[:SIDES, :SIDES], gram[:SIDES, SIDES:], gram[SIDES:, SIDES:]
    packed = [rr[:8], rr[8:], ri[:8], ri[8:], ii[:8], ii[8:], jnp.zeros((8, 160), F32)]
    message = jnp.concatenate([w[...] * i0, jnp.concatenate(packed, axis=1)], axis=0)
    for g in range(GRP):
        out[g] = message


def gram_sum(own, out):
    total = own[0]
    for g in range(1, GRP):
        total = total + own[g]
    for g in range(GRP):
        out[g] = total


def second_apply(
    place, mom, own_i, other_i, own_s, other_s, res_ref, img_ref, *more
):
    tile, (out, sol1, res1, dir1, gram1) = more[:PIECES], more[PIECES:]
    total = jnp.sum(mom[...], axis=0)
    rr, ri, ii = unpack(total, 0), unpack(total, 1), unpack(total, 2)
    step = spd_solve(ri, rr)
    cross = hdot(step, ri, ((0,), (1,)))
    new = rr - cross - cross.T + hdot(step, hdot(ii, step, ((1,), (0,))), ((0,), (0,)))
    mix = spd_solve(rr, new)
    gram1[...] = new
    r0, i0 = res_ref[...], img_ref[...]
    sol1[...] = hdot(step, r0, ((0,), (0,)))
    r1 = r0 - hdot(step, i0, ((0,), (0,)))
    res1[...] = r1
    dir1[...] = r1 + hdot(mix, r0, ((0,), (0,)))
    rows = lax.broadcasted_iota(jnp.int32, (SIDES, SIDES), 0)
    lanes = lax.broadcasted_iota(jnp.int32, (SIDES, SIDES), 1)
    coef = jnp.concatenate([jnp.where(rows == lanes, 1.0, 0.0) + mix, -step], axis=0)
    vec = []
    for i_ref, s_ref in ((own_i, own_s), (other_i, other_s)):
        for g in range(GRP):
            wr = s_ref[g, :SIDES, :].astype(F32) + s_ref[g, SIDES:, :].astype(F32)
            both = jnp.concatenate([wr, i_ref[g]], axis=0)
            vec.append(hdot(coef, both, ((0,), (0,))).astype(BF16))
    total = jnp.zeros((SIDES, ROWS), F32)
    for j in range(len(vec)):
        kernel = tile[j * PT // PIECE][pl.ds(j * PT % PIECE, PT), :]
        total += jnp.dot(vec[j], kernel, preferred_element_type=F32)
    place_blocks(place, out, total)


def second_image(parts, base, w, out, image):
    total = parts[0]
    for g in range(1, DEPTH):
        total = total + parts[g]
    img = base[...] + w[...] * total
    image[...] = img
    gram = hdot(base[...], img, ((1,), (1,)))
    gram = 0.5 * (gram + gram.T)
    high = gram.astype(BF16).astype(F32)
    rows = lax.broadcasted_iota(jnp.int32, (SIDES, SIDES), 0)
    lanes = lax.broadcasted_iota(jnp.int32, (SIDES, SIDES), 1)
    gram = jnp.where(rows <= lanes, high, gram - high)
    top = jnp.concatenate([gram[i : i + 1] for i in range(8)], axis=1)
    bottom = jnp.concatenate([gram[i : i + 1] for i in range(8, 16)], axis=1)
    packed = jnp.concatenate([top, bottom], axis=0).astype(BF16)
    out[...] = jnp.broadcast_to(packed[None], out.shape)


def finish(grams, gram1, sol1, res1, dir1, img1, sol, res):
    total = jnp.sum(grams[...].astype(F32), axis=0)
    gram = jnp.concatenate(
        [total[i // 8 : i // 8 + 1, 16 * (i % 8) : 16 * (i % 8) + 16] for i in range(16)], axis=0
    )
    rows = lax.broadcasted_iota(jnp.int32, (SIDES, SIDES), 0)
    lanes = lax.broadcasted_iota(jnp.int32, (SIDES, SIDES), 1)
    gram = gram + jnp.where(rows == lanes, 0.0, gram.T)
    step = spd_solve(gram, gram1[...])
    sol[...] = sol1[...] + hdot(step, dir1[...], ((0,), (0,)))
    res[...] = res1[...] - hdot(step, img1[...], ((0,), (0,)))


def shape(*dims, dtype=F32):
    return jax.ShapeDtypeStruct(dims, dtype)


def call(body, out, vmem=8, **more):
    return pl.pallas_call(
        body,
        out_shape=out,
        compiler_params=pltpu.CompilerParams(vmem_limit_bytes=int(vmem * 2**20)),
        **more,
    )


def block(*dims, at=None):
    return pl.BlockSpec(dims, lambda i: at or (0,) * len(dims))


def swap_along_z(array, k):
    return lax.ppermute(array, "z", [(i, i ^ k) for i in range(DEPTH)])


def swap_cores(array):
    return lax.ppermute(array, "core", ((0, 1), (1, 0)))


def per_device(embeddings, latent, list_of, rank_of, probes):
    resident = pl.BlockSpec(memory_space=pltpu.VMEM)
    anywhere = pl.BlockSpec(memory_space=pl.ANY)
    msg_c, points, res0, w = call(
        prepare,
        (
            shape(GRP, D + 2 * SIDES, PT, dtype=BF16),
            shape(D, PT, dtype=BF16),
            shape(SIDES, PT),
            shape(1, PT),
        ),
        vmem=VMEM_ALL,
        in_specs=[anywhere] * 5,
        scratch_shapes=[
            pltpu.VMEM((1, PT), F32),
            pltpu.VMEM((1, PT), jnp.int32),
            pltpu.VMEM((1, PT), jnp.int32),
            pltpu.VMEM((SIDES - 1, PT), F32),
            pltpu.SemaphoreType.DMA((5,)),
        ],
        name="prepare",
    )(embeddings, latent[None, :], list_of[None, :], rank_of[None, :], probes)
    own_c = lax.all_to_all(msg_c, GROUP_C, 0, 0, tiled=True)
    pair = jnp.concatenate([points, swap_along_z(points, 1)], axis=1)
    all_r = [pair] + [swap_along_z(pair, k) for k in range(2, DEPTH, 2)]
    own_c, all_r = lax.optimization_barrier((own_c, all_r))
    other_c = swap_cores(own_c)

    place = lax.axis_index("z").astype(jnp.int32)[None]
    half_tile = [pltpu.VMEM((PIECE, ROWS), BF16)] * (PIECES // 2)
    scratch = [pltpu.VMEM((HALF, AUG), BF16), pltpu.VMEM((SIDES, HALF), BF16)]
    in_vmem = pl.BlockSpec(memory_space=pltpu.VMEM)
    in_smem = pl.BlockSpec(memory_space=pltpu.SMEM)
    part, right, *tile = call(
        first_half,
        (shape(SIDES, ROWS), shape(AUG, ROWS, dtype=BF16), *half_tile),
        in_specs=[in_vmem] * (1 + PAIRS),
        out_specs=[in_vmem] * (2 + PIECES // 2),
        scratch_shapes=scratch,
        name="first_half",
    )(own_c, *all_r)
    part, *more = call(
        second_half,
        (shape(DEPTH, SIDES, PT), *half_tile),
        in_specs=[in_smem] + [in_vmem] * 3,
        out_specs=[in_vmem] * (1 + PIECES // 2),
        scratch_shapes=scratch,
        name="second_half",
    )(place, other_c, right, part)
    tile = tile + more
    part = lax.all_to_all(part, "z", 0, 0, tiled=True)

    message, img0 = call(
        first_image, (shape(GRP, SIDES + 8, PT), shape(SIDES, PT)), name="first_image"
    )(part, res0, w)
    own_i = lax.all_to_all(message, GROUP_C, 0, 0, tiled=True)
    other_i = swap_cores(own_i)
    mom = call(
        gram_sum,
        shape(GRP, 8, 128),
        grid=(1,),
        in_specs=[block(GRP, 8, 128, at=(0, 2, 0))],
        out_specs=block(GRP, 8, 128),
        name="gram_sum",
    )(own_i)
    mom = lax.all_to_all(mom, GROUP_R, 0, 0, tiled=True)

    images = block(GRP, SIDES, PT)
    scaled = block(GRP, 2 * SIDES, PT, at=(0, 2, 0))
    own = block(SIDES, PT)
    part, sol1, res1, dir1, gram1 = call(
        second_apply,
        (
            shape(DEPTH, SIDES, PT),
            shape(SIDES, PT),
            shape(SIDES, PT),
            shape(SIDES, PT),
            shape(SIDES, SIDES),
        ),
        grid=(1,),
        in_specs=[in_smem, block(GRP, 8, 128), images, images, scaled, scaled, own, own] + [resident] * PIECES,
        out_specs=(block(DEPTH, SIDES, PT), own, own, own, block(SIDES, SIDES)),
        name="second_apply",
    )(place, mom, own_i, other_i, own_c, other_c, res0, img0, *tile)
    part = lax.all_to_all(part, "z", 0, 0, tiled=True)

    grams, img1 = call(
        second_image, (shape(256, 2, 128, dtype=BF16), shape(SIDES, PT)), name="second_image"
    )(part, dir1, w)
    grams = lax.all_to_all(grams, ALL, 0, 0, tiled=True)
    return call(finish, (shape(SIDES, PT), shape(SIDES, PT)), name="finish")(
        grams, gram1, sol1, res1, dir1, img1
    )


def solution(mesh):
    grid = Mesh(mesh.devices.reshape(4, 2, 8, 4), ALL)
    in_specs = (P(None, ALL), P(ALL), P(ALL), P(ALL), P(None, ALL))
    return jax.shard_map(
        per_device,
        mesh=grid,
        in_specs=in_specs,
        out_specs=(P(None, ALL), P(None, ALL)),
        check_vma=False,
    )
```

```python
import jax
import jax.numpy as jnp
from jax import lax
from jax.experimental import pallas as pl
from jax.experimental.pallas import tpu as pltpu
from jax.sharding import Mesh
from jax.sharding import PartitionSpec as P

D = 64
SIDES = 16
LIST_LEN = 8
PT = 256
RIDGE = 0.01
GAMMA = 2.0 / D
ALL = ("y", "core", "z", "x")
GROUP_C = ("y", "x")
GROUP_LAST = ("y", "core", "x")
GRP = 16
DEPTH = 8
PAIRS = DEPTH // 2
HALF = GRP * PT
COLS = 2 * HALF
ROWS = DEPTH * PT
AUG = 80
VMEM_ALL = 60
PIECES = 16
PIECE = COLS // PIECES

F32 = jnp.float32
BF16 = jnp.bfloat16


def hdot(a, b, dims):
    return lax.dot_general(
        a, b, (dims, ((), ())), precision=lax.Precision.HIGHEST, preferred_element_type=F32
    )


def split3(v):
    hi = v.astype(BF16).astype(F32)
    mid = (v - hi).astype(BF16).astype(F32)
    lo = (v - hi - mid).astype(BF16).astype(F32)
    return hi, mid, lo


def spd_solve(gram, right):
    n = gram.shape[0]
    rows = lax.broadcasted_iota(jnp.int32, right.shape, 0)
    gram = 0.5 * (gram + gram.T)
    columns = [jnp.broadcast_to(gram[:, k : k + 1], right.shape) for k in range(n)]
    diagonal = jnp.ones(right.shape, F32)
    for k in range(n):
        pivot = columns[k][k : k + 1, :]
        scale = 1.0 / pivot
        factor = jnp.where(rows == k, 0.0, columns[k])
        diagonal = jnp.where(rows == k, scale, diagonal)
        for j in range(k + 1, n):
            columns[j] = columns[j] - factor * (columns[j][k : k + 1, :] * scale)
        right = right - factor * (right[k : k + 1, :] * scale)
    return right * diagonal


def prepare(
    emb_in, latent_in, list_in, rank_in, probes_in,
    msg_c, scaled_own, resid, weight,
    emb, latent, list_of, rank_of, probes, sems,
):
    pairs = (
        (latent_in, latent), (list_in, list_of), (rank_in, rank_of), (probes_in, probes), (emb_in, emb),
    )
    copies = [pltpu.make_async_copy(a, b, sems.at[i]) for i, (a, b) in enumerate(pairs)]
    for copy in copies:
        copy.start()
    for copy in copies[:3]:
        copy.wait()
    row = jnp.concatenate(
        [
            latent[...],
            list_of[...].astype(F32),
            rank_of[...].astype(F32),
            jnp.zeros((5, PT), F32),
        ],
        axis=0,
    )
    col = row.T
    same = col[:, 1:2] == row[1:2, :]
    highest = jnp.max(jnp.where(same, col[:, 0:1], -jnp.inf), axis=0, keepdims=True)
    shifted = jnp.exp(row[0:1, :] - highest)
    shifted_col = jnp.broadcast_to(shifted, (8, PT)).T[:, 0:1]
    gradient = jnp.ones((1, PT), F32)
    curvature = jnp.zeros((1, PT), F32)
    for k in range(LIST_LEN):
        held = jnp.where(col[:, 2:3] >= k, shifted_col, 0.0)
        totals = jnp.sum(jnp.where(same, held, 0.0), axis=0, keepdims=True)
        chance = shifted / totals
        active = row[2:3, :] >= k
        gradient = gradient - jnp.where(active, chance, 0.0)
        curvature = curvature + jnp.where(active, chance * (1.0 - chance), 0.0)
    w = jnp.sqrt(curvature + RIDGE)
    copies[3].wait()
    copies[4].wait()
    r0 = jnp.concatenate([gradient, probes[...]], axis=0)
    resid[...] = r0
    weight[...] = w
    scaled = w * r0
    high = scaled.astype(BF16)
    low = (scaled - high.astype(F32)).astype(BF16)
    scaled_own[...] = high
    for g in range(GRP):
        msg_c[g, :D, :] = emb[...]
        msg_c[g, D : D + SIDES, :] = high
        msg_c[g, D + SIDES :, :] = low


def norm_rows(points):
    sq = -GAMMA * jnp.sum(points * points, axis=0, keepdims=True)
    return jnp.concatenate(split3(sq), axis=0)


def half_apply(c_ref, right, tile, left, vec):
    ones = jnp.ones((3, PT), F32)
    zeros = jnp.zeros((AUG - D - 6, PT), F32)
    for g in range(GRP):
        at = slice(g * PT, (g + 1) * PT)
        points = c_ref[g, :D, :].astype(F32)
        rows = jnp.concatenate([points, ones, norm_rows(points), zeros], axis=0)
        left[at, :] = rows.astype(BF16).T
        vec[:, at] = c_ref[g, D : D + SIDES, :]
    step = 256
    total = jnp.zeros((SIDES, ROWS), F32)
    for j in range(HALF // step):
        at = slice(j * step, (j + 1) * step)
        exponent = jnp.dot(left[at, :], right[...], preferred_element_type=F32)
        kernel = jnp.exp(exponent).astype(BF16)
        tile[j * step // PIECE][pl.ds(j * step % PIECE, step), :] = kernel
        total += jnp.dot(vec[:, at], kernel, preferred_element_type=F32)
    return total


def first_half(c_ref, *more):
    r_refs, out, right, more = more[:PAIRS], more[PAIRS], more[PAIRS + 1], more[PAIRS + 2 :]
    ones = jnp.ones((3, PT), F32)
    zeros = jnp.zeros((AUG - D - 6, PT), F32)
    for k in range(DEPTH):
        points = r_refs[k // 2][:, k % 2 * PT : (k % 2 + 1) * PT].astype(F32)
        rows = [points * (2.0 * GAMMA), norm_rows(points), ones, zeros]
        right[:, k * PT : (k + 1) * PT] = jnp.concatenate(rows, axis=0).astype(BF16)
    out[...] = half_apply(c_ref, right, more[: PIECES // 2], *more[PIECES // 2 :])


def second_half(place, c_ref, right, before, out, *more):
    total = half_apply(c_ref, right, more[: PIECES // 2], *more[PIECES // 2 :])
    total = total + before[...]
    for k in range(DEPTH):
        out[lax.bitwise_xor(place[0], k)] = total[:, k * PT : (k + 1) * PT]


def unpack(total, n):
    return jnp.concatenate(
        [total[:, 32 * n : 32 * n + 16], total[:, 32 * n + 16 : 32 * n + 32]], axis=0
    )


def first_image(parts, base, w, out, image, weighted):
    total = parts[0]
    for g in range(1, DEPTH):
        total = total + parts[g]
    r0 = base[...]
    i0 = r0 + w[...] * total
    image[...] = i0
    both = jnp.concatenate([r0, i0], axis=0)
    gram = hdot(both, both, ((1,), (1,)))
    rr, ri, ii = gram[:SIDES, :SIDES], gram[:SIDES, SIDES:], gram[SIDES:, SIDES:]
    packed = [rr[:8], rr[8:], ri[:8], ri[8:], ii[:8], ii[8:], jnp.zeros((8, 160), F32)]
    weighted[...] = w[...] * i0
    message = jnp.concatenate([w[...] * i0, jnp.concatenate(packed, axis=1)], axis=0)
    for g in range(GRP):
        out[g] = message


def gram_sum(own, other, scaled, weighted, out):
    total = own[0] + other[0]
    for g in range(1, GRP):
        total = total + (own[g] + other[g])
    high, mid, low = split3(total)
    grams = [
        jnp.concatenate([high, mid], axis=1),
        jnp.concatenate([low, jnp.zeros((8, PT - 128), F32)], axis=1),
    ]
    message = jnp.concatenate([weighted[...]] + grams, axis=0).astype(BF16)
    for g in range(DEPTH):
        out[g, :SIDES, :] = scaled[...]
        out[g, SIDES:, :] = message


def second_apply(place, along_z, own_i, other_i, own_s, other_s, *more):
    (res_ref, img_ref), more = more[:2], more[2:]
    tile, (out, sol1, res1, dir1, gram1) = more[:PIECES], more[PIECES:]
    total = along_z[0, 2 * SIDES :, :].astype(F32)
    for g in range(1, DEPTH):
        total = total + along_z[g, 2 * SIDES :, :].astype(F32)
    total = total[:8, :128] + (total[:8, 128:] + total[8:, :128])
    rr, ri, ii = unpack(total, 0), unpack(total, 1), unpack(total, 2)
    step = spd_solve(ri, rr)
    cross = hdot(step, ri, ((0,), (1,)))
    new = rr - cross - cross.T + hdot(step, hdot(ii, step, ((1,), (0,))), ((0,), (0,)))
    mix = spd_solve(rr, new)
    gram1[...] = new
    r0, i0 = res_ref[...], img_ref[...]
    sol1[...] = hdot(step, r0, ((0,), (0,)))
    r1 = r0 - hdot(step, i0, ((0,), (0,)))
    res1[...] = r1
    d1 = r1 + hdot(mix, r0, ((0,), (0,)))
    dir1[...] = d1
    rows = lax.broadcasted_iota(jnp.int32, (SIDES, SIDES), 0)
    lanes = lax.broadcasted_iota(jnp.int32, (SIDES, SIDES), 1)
    coef = jnp.concatenate([jnp.where(rows == lanes, 1.0, 0.0) + mix, -step], axis=0)
    vec = []
    for i_ref, s_ref in ((own_i, own_s), (other_i, other_s)):
        for g in range(GRP):
            wr = s_ref[g, :SIDES, :].astype(F32) + s_ref[g, SIDES:, :].astype(F32)
            both = jnp.concatenate([wr, i_ref[g]], axis=0)
            vec.append(hdot(coef, both, ((0,), (0,))).astype(BF16))
    total = jnp.zeros((SIDES, ROWS), F32)
    for j in range(len(vec)):
        kernel = tile[j * PT // PIECE][pl.ds(j * PT % PIECE, PT), :]
        total += jnp.dot(vec[j], kernel, preferred_element_type=F32)
    weighted = []
    for k in range(DEPTH):
        both = along_z[lax.bitwise_xor(place[0], k), : 2 * SIDES, :].astype(F32)
        weighted.append(hdot(coef, both, ((0,), (0,))))
    gram = hdot(d1, d1, ((1,), (1,)))
    gram = gram + hdot(jnp.concatenate(weighted, axis=1), total, ((1,), (1,)))
    gram = jnp.concatenate([gram[:8], gram[8:], jnp.zeros((8, PT - 32), F32)], axis=1)
    for k in range(DEPTH):
        part = total[:, k * PT : (k + 1) * PT]
        out[lax.bitwise_xor(place[0], k)] = jnp.concatenate([part, gram], axis=0)


def second_image(parts, base, w, out, image):
    total = parts[0]
    for g in range(1, DEPTH):
        total = total + parts[g]
    image[...] = base[...] + w[...] * total[:SIDES]
    gram = unpack(total[SIDES:], 0)
    top = jnp.concatenate([gram[i : i + 1] for i in range(8)], axis=1)
    bottom = jnp.concatenate([gram[i : i + 1] for i in range(8, 16)], axis=1)
    packed = jnp.concatenate([top, bottom], axis=0)
    out[...] = jnp.broadcast_to(packed[None], out.shape)


def finish(grams, gram1, sol1, res1, dir1, img1, sol, res):
    total = jnp.sum(grams[...], axis=0)
    gram = jnp.concatenate(
        [total[i // 8 : i // 8 + 1, 16 * (i % 8) : 16 * (i % 8) + 16] for i in range(16)], axis=0
    )
    step = spd_solve(gram, gram1[...])
    sol[...] = sol1[...] + hdot(step, dir1[...], ((0,), (0,)))
    res[...] = res1[...] - hdot(step, img1[...], ((0,), (0,)))


def shape(*dims, dtype=F32):
    return jax.ShapeDtypeStruct(dims, dtype)


def call(body, out, vmem=8, **more):
    return pl.pallas_call(
        body,
        out_shape=out,
        compiler_params=pltpu.CompilerParams(vmem_limit_bytes=int(vmem * 2**20)),
        **more,
    )


def block(*dims, at=None):
    return pl.BlockSpec(dims, lambda i: at or (0,) * len(dims))


def swap_along_z(array, k):
    return lax.ppermute(array, "z", [(i, i ^ k) for i in range(DEPTH)])


def swap_cores(array):
    return lax.ppermute(array, "core", ((0, 1), (1, 0)))


def per_device(embeddings, latent, list_of, rank_of, probes):
    resident = pl.BlockSpec(memory_space=pltpu.VMEM)
    anywhere = pl.BlockSpec(memory_space=pl.ANY)
    msg_c, scaled_own, res0, w = call(
        prepare,
        (
            shape(GRP, D + 2 * SIDES, PT, dtype=BF16),
            shape(SIDES, PT, dtype=BF16),
            shape(SIDES, PT),
            shape(1, PT),
        ),
        vmem=VMEM_ALL,
        in_specs=[anywhere] * 5,
        scratch_shapes=[
            pltpu.VMEM((D, PT), BF16),
            pltpu.VMEM((1, PT), F32),
            pltpu.VMEM((1, PT), jnp.int32),
            pltpu.VMEM((1, PT), jnp.int32),
            pltpu.VMEM((SIDES - 1, PT), F32),
            pltpu.SemaphoreType.DMA((5,)),
        ],
        name="prepare",
    )(embeddings, latent[None, :], list_of[None, :], rank_of[None, :], probes)
    own_c = lax.all_to_all(msg_c, GROUP_C, 0, 0, tiled=True)
    pair = jnp.concatenate([embeddings, swap_along_z(embeddings, 1)], axis=1)
    all_r = [pair] + [swap_along_z(pair, k) for k in range(2, DEPTH, 2)]
    own_c, all_r = lax.optimization_barrier((own_c, all_r))
    other_c = swap_cores(own_c)

    place = lax.axis_index("z").astype(jnp.int32)[None]
    half_tile = [pltpu.VMEM((PIECE, ROWS), BF16)] * (PIECES // 2)
    scratch = [pltpu.VMEM((HALF, AUG), BF16), pltpu.VMEM((SIDES, HALF), BF16)]
    in_vmem = pl.BlockSpec(memory_space=pltpu.VMEM)
    in_smem = pl.BlockSpec(memory_space=pltpu.SMEM)
    part, right, *tile = call(
        first_half,
        (shape(SIDES, ROWS), shape(AUG, ROWS, dtype=BF16), *half_tile),
        in_specs=[in_vmem] * (1 + PAIRS),
        out_specs=[in_vmem] * (2 + PIECES // 2),
        scratch_shapes=scratch,
        name="first_half",
    )(own_c, *all_r)
    part, *more = call(
        second_half,
        (shape(DEPTH, SIDES, PT), *half_tile),
        in_specs=[in_smem] + [in_vmem] * 3,
        out_specs=[in_vmem] * (1 + PIECES // 2),
        scratch_shapes=scratch,
        name="second_half",
    )(place, other_c, right, part)
    tile = tile + more
    part = lax.all_to_all(part, "z", 0, 0, tiled=True)

    message, img0, weighted = call(
        first_image,
        (shape(GRP, SIDES + 8, PT), shape(SIDES, PT), shape(SIDES, PT)),
        name="first_image",
    )(part, res0, w)
    own_i = lax.all_to_all(message, GROUP_C, 0, 0, tiled=True)
    other_i = swap_cores(own_i)
    grams = block(GRP, 8, 128, at=(0, 2, 0))
    own = block(SIDES, PT)
    along_z = call(
        gram_sum,
        shape(DEPTH, 3 * SIDES, PT, dtype=BF16),
        grid=(1,),
        in_specs=[grams, grams, own, own],
        out_specs=block(DEPTH, 3 * SIDES, PT),
        name="gram_sum",
    )(own_i, other_i, scaled_own, weighted)
    along_z = lax.all_to_all(along_z, "z", 0, 0, tiled=True)

    images = block(GRP, SIDES, PT)
    scaled = block(GRP, 2 * SIDES, PT, at=(0, 2, 0))
    part, sol1, res1, dir1, gram1 = call(
        second_apply,
        (
            shape(DEPTH, SIDES + 8, PT),
            shape(SIDES, PT),
            shape(SIDES, PT),
            shape(SIDES, PT),
            shape(SIDES, SIDES),
        ),
        grid=(1,),
        in_specs=[in_smem, block(DEPTH, 3 * SIDES, PT)]
        + [images, images, scaled, scaled]
        + [own, own] + [resident] * PIECES,
        out_specs=(block(DEPTH, SIDES + 8, PT), own, own, own, block(SIDES, SIDES)),
        name="second_apply",
    )(place, along_z, own_i, other_i, own_c, other_c, res0, img0, *tile)
    part = lax.all_to_all(part, "z", 0, 0, tiled=True)

    grams, img1 = call(
        second_image, (shape(2 * GRP, 2, 128), shape(SIDES, PT)), name="second_image"
    )(part, dir1, w)
    grams = lax.all_to_all(grams, GROUP_LAST, 0, 0, tiled=True)
    return call(finish, (shape(SIDES, PT), shape(SIDES, PT)), name="finish")(
        grams, gram1, sol1, res1, dir1, img1
    )


def solution(mesh):
    grid = Mesh(mesh.devices.reshape(4, 2, 8, 4), ALL)
    in_specs = (P(None, ALL), P(ALL), P(ALL), P(ALL), P(None, ALL))
    return jax.shard_map(
        per_device,
        mesh=grid,
        in_specs=in_specs,
        out_specs=(P(None, ALL), P(None, ALL)),
        check_vma=False,
    )
```

```python
import jax
import jax.numpy as jnp
from jax import lax
from jax.experimental import pallas as pl
from jax.experimental.pallas import tpu as pltpu
from jax.sharding import Mesh
from jax.sharding import PartitionSpec as P

D = 64
SIDES = 16
LIST_LEN = 8
PT = 256
RIDGE = 0.01
GAMMA = 2.0 / D
ALL = ("y", "core", "z", "x")
GROUP_C = ("y", "x")
GROUP_LAST = ("y", "core", "x")
GRP = 16
DEPTH = 8
PAIRS = DEPTH // 2
ORDER = (0, 1, 6, 7, 2, 3, 4, 5)
HALF = GRP * PT
COLS = 2 * HALF
ROWS = DEPTH * PT
AUG = 80
VMEM_ALL = 60
PIECES = 16
PIECE = COLS // PIECES

F32 = jnp.float32
BF16 = jnp.bfloat16


def hdot(a, b, dims):
    return lax.dot_general(
        a, b, (dims, ((), ())), precision=lax.Precision.HIGHEST, preferred_element_type=F32
    )


def split3(v):
    hi = v.astype(BF16).astype(F32)
    mid = (v - hi).astype(BF16).astype(F32)
    lo = (v - hi - mid).astype(BF16).astype(F32)
    return hi, mid, lo


def spd_solve(gram, right):
    n = gram.shape[0]
    rows = lax.broadcasted_iota(jnp.int32, right.shape, 0)
    gram = 0.5 * (gram + gram.T)
    columns = [jnp.broadcast_to(gram[:, k : k + 1], right.shape) for k in range(n)]
    diagonal = jnp.ones(right.shape, F32)
    for k in range(n):
        pivot = columns[k][k : k + 1, :]
        scale = 1.0 / pivot
        factor = jnp.where(rows == k, 0.0, columns[k])
        diagonal = jnp.where(rows == k, scale, diagonal)
        for j in range(k + 1, n):
            columns[j] = columns[j] - factor * (columns[j][k : k + 1, :] * scale)
        right = right - factor * (right[k : k + 1, :] * scale)
    return right * diagonal


def prepare(
    emb_in, latent_in, list_in, rank_in, probes_in,
    msg_c, scaled_own, resid, weight,
    emb, latent, list_of, rank_of, probes, sems,
):
    pairs = (
        (latent_in, latent), (list_in, list_of), (rank_in, rank_of), (probes_in, probes), (emb_in, emb),
    )
    copies = [pltpu.make_async_copy(a, b, sems.at[i]) for i, (a, b) in enumerate(pairs)]
    for copy in copies:
        copy.start()
    for copy in copies[:3]:
        copy.wait()
    row = jnp.concatenate(
        [
            latent[...],
            list_of[...].astype(F32),
            rank_of[...].astype(F32),
            jnp.zeros((5, PT), F32),
        ],
        axis=0,
    )
    col = row.T
    same = col[:, 1:2] == row[1:2, :]
    highest = jnp.max(jnp.where(same, col[:, 0:1], -jnp.inf), axis=0, keepdims=True)
    shifted = jnp.exp(row[0:1, :] - highest)
    shifted_col = jnp.broadcast_to(shifted, (8, PT)).T[:, 0:1]
    gradient = jnp.ones((1, PT), F32)
    curvature = jnp.zeros((1, PT), F32)
    for k in range(LIST_LEN):
        held = jnp.where(col[:, 2:3] >= k, shifted_col, 0.0)
        totals = jnp.sum(jnp.where(same, held, 0.0), axis=0, keepdims=True)
        chance = shifted / totals
        active = row[2:3, :] >= k
        gradient = gradient - jnp.where(active, chance, 0.0)
        curvature = curvature + jnp.where(active, chance * (1.0 - chance), 0.0)
    w = jnp.sqrt(curvature + RIDGE)
    copies[3].wait()
    copies[4].wait()
    r0 = jnp.concatenate([gradient, probes[...]], axis=0)
    resid[...] = r0
    weight[...] = w
    scaled = w * r0
    high = scaled.astype(BF16)
    low = (scaled - high.astype(F32)).astype(BF16)
    scaled_own[...] = high
    for g in range(GRP):
        msg_c[g, :D, :] = emb[...]
        msg_c[g, D : D + SIDES, :] = high
        msg_c[g, D + SIDES :, :] = low


def norm_rows(points):
    sq = -GAMMA * jnp.sum(points * points, axis=0, keepdims=True)
    return jnp.concatenate(split3(sq), axis=0)


def half_apply(c_ref, right, tile, left, vec):
    ones = jnp.ones((3, PT), F32)
    zeros = jnp.zeros((AUG - D - 6, PT), F32)
    for g in range(GRP):
        at = slice(g * PT, (g + 1) * PT)
        points = c_ref[g, :D, :].astype(F32)
        rows = jnp.concatenate([points, ones, norm_rows(points), zeros], axis=0)
        left[at, :] = rows.astype(BF16).T
        vec[:, at] = c_ref[g, D : D + SIDES, :]
    step = 256
    total = jnp.zeros((SIDES, ROWS), F32)
    for j in range(HALF // step):
        at = slice(j * step, (j + 1) * step)
        exponent = jnp.dot(left[at, :], right[...], preferred_element_type=F32)
        kernel = jnp.exp(exponent).astype(BF16)
        tile[j * step // PIECE][pl.ds(j * step % PIECE, step), :] = kernel
        total += jnp.dot(vec[:, at], kernel, preferred_element_type=F32)
    return total


def first_half(c_ref, *more):
    r_refs, out, right, more = more[:PAIRS], more[PAIRS], more[PAIRS + 1], more[PAIRS + 2 :]
    ones = jnp.ones((3, PT), F32)
    zeros = jnp.zeros((AUG - D - 6, PT), F32)
    for k in range(DEPTH):
        points = r_refs[k // 2][:, k % 2 * PT : (k % 2 + 1) * PT].astype(F32)
        rows = [points * (2.0 * GAMMA), norm_rows(points), ones, zeros]
        right[:, k * PT : (k + 1) * PT] = jnp.concatenate(rows, axis=0).astype(BF16)
    out[...] = half_apply(c_ref, right, more[: PIECES // 2], *more[PIECES // 2 :])


def second_half(place, c_ref, right, before, out, *more):
    total = half_apply(c_ref, right, more[: PIECES // 2], *more[PIECES // 2 :])
    total = total + before[...]
    for k in range(DEPTH):
        out[lax.bitwise_xor(place[0], ORDER[k])] = total[:, k * PT : (k + 1) * PT]


def unpack(total, n):
    return jnp.concatenate(
        [total[:, 32 * n : 32 * n + 16], total[:, 32 * n + 16 : 32 * n + 32]], axis=0
    )


def first_image(parts, base, w, out, image, weighted):
    total = parts[0]
    for g in range(1, DEPTH):
        total = total + parts[g]
    r0 = base[...]
    i0 = r0 + w[...] * total
    image[...] = i0
    both = jnp.concatenate([r0, i0], axis=0)
    gram = hdot(both, both, ((1,), (1,)))
    rr, ri, ii = gram[:SIDES, :SIDES], gram[:SIDES, SIDES:], gram[SIDES:, SIDES:]
    packed = [rr[:8], rr[8:], ri[:8], ri[8:], ii[:8], ii[8:], jnp.zeros((8, 160), F32)]
    weighted[...] = w[...] * i0
    message = jnp.concatenate([w[...] * i0, jnp.concatenate(packed, axis=1)], axis=0)
    for g in range(GRP):
        out[g] = message


def gram_sum(own, other, scaled, weighted, out):
    total = own[0] + other[0]
    for g in range(1, GRP):
        total = total + (own[g] + other[g])
    high, mid, low = split3(total)
    grams = [
        jnp.concatenate([high, mid], axis=1),
        jnp.concatenate([low, jnp.zeros((8, PT - 128), F32)], axis=1),
    ]
    message = jnp.concatenate([weighted[...]] + grams, axis=0).astype(BF16)
    for g in range(DEPTH):
        out[g, :SIDES, :] = scaled[...]
        out[g, SIDES:, :] = message


def second_apply(place, along_z, own_i, other_i, own_s, other_s, *more):
    (res_ref, img_ref), more = more[:2], more[2:]
    tile, (out, sol1, res1, dir1, gram1) = more[:PIECES], more[PIECES:]
    total = along_z[0, 2 * SIDES :, :].astype(F32)
    for g in range(1, DEPTH):
        total = total + along_z[g, 2 * SIDES :, :].astype(F32)
    total = total[:8, :128] + (total[:8, 128:] + total[8:, :128])
    rr, ri, ii = unpack(total, 0), unpack(total, 1), unpack(total, 2)
    step = spd_solve(ri, rr)
    cross = hdot(step, ri, ((0,), (1,)))
    new = rr - cross - cross.T + hdot(step, hdot(ii, step, ((1,), (0,))), ((0,), (0,)))
    mix = spd_solve(rr, new)
    gram1[...] = new
    r0, i0 = res_ref[...], img_ref[...]
    sol1[...] = hdot(step, r0, ((0,), (0,)))
    r1 = r0 - hdot(step, i0, ((0,), (0,)))
    res1[...] = r1
    d1 = r1 + hdot(mix, r0, ((0,), (0,)))
    dir1[...] = d1
    rows = lax.broadcasted_iota(jnp.int32, (SIDES, SIDES), 0)
    lanes = lax.broadcasted_iota(jnp.int32, (SIDES, SIDES), 1)
    coef = jnp.concatenate([jnp.where(rows == lanes, 1.0, 0.0) + mix, -step], axis=0)
    vec = []
    for i_ref, s_ref in ((own_i, own_s), (other_i, other_s)):
        for g in range(GRP):
            wr = s_ref[g, :SIDES, :].astype(F32) + s_ref[g, SIDES:, :].astype(F32)
            both = jnp.concatenate([wr, i_ref[g]], axis=0)
            vec.append(hdot(coef, both, ((0,), (0,))).astype(BF16))
    total = jnp.zeros((SIDES, ROWS), F32)
    for j in range(len(vec)):
        kernel = tile[j * PT // PIECE][pl.ds(j * PT % PIECE, PT), :]
        total += jnp.dot(vec[j], kernel, preferred_element_type=F32)
    weighted = []
    for k in range(DEPTH):
        both = along_z[lax.bitwise_xor(place[0], ORDER[k]), : 2 * SIDES, :].astype(F32)
        weighted.append(hdot(coef, both, ((0,), (0,))))
    gram = hdot(d1, d1, ((1,), (1,)))
    gram = gram + hdot(jnp.concatenate(weighted, axis=1), total, ((1,), (1,)))
    gram = jnp.concatenate([gram[:8], gram[8:], jnp.zeros((8, PT - 32), F32)], axis=1)
    for k in range(DEPTH):
        part = total[:, k * PT : (k + 1) * PT]
        out[lax.bitwise_xor(place[0], ORDER[k])] = jnp.concatenate([part, gram], axis=0)


def second_image(parts, base, w, out, image):
    total = parts[0]
    for g in range(1, DEPTH):
        total = total + parts[g]
    image[...] = base[...] + w[...] * total[:SIDES]
    gram = unpack(total[SIDES:], 0)
    top = jnp.concatenate([gram[i : i + 1] for i in range(8)], axis=1)
    bottom = jnp.concatenate([gram[i : i + 1] for i in range(8, 16)], axis=1)
    packed = jnp.concatenate([top, bottom], axis=0)
    out[...] = jnp.broadcast_to(packed[None], out.shape)


def finish(grams, gram1, sol1, res1, dir1, img1, sol, res):
    total = jnp.sum(grams[...], axis=0)
    gram = jnp.concatenate(
        [total[i // 8 : i // 8 + 1, 16 * (i % 8) : 16 * (i % 8) + 16] for i in range(16)], axis=0
    )
    step = spd_solve(gram, gram1[...])
    sol[...] = sol1[...] + hdot(step, dir1[...], ((0,), (0,)))
    res[...] = res1[...] - hdot(step, img1[...], ((0,), (0,)))


def shape(*dims, dtype=F32):
    return jax.ShapeDtypeStruct(dims, dtype)


def call(body, out, vmem=8, **more):
    return pl.pallas_call(
        body,
        out_shape=out,
        compiler_params=pltpu.CompilerParams(vmem_limit_bytes=int(vmem * 2**20)),
        **more,
    )


def block(*dims, at=None):
    return pl.BlockSpec(dims, lambda i: at or (0,) * len(dims))


def swap_along_z(array, k):
    return lax.ppermute(array, "z", [(i, i ^ k) for i in range(DEPTH)])


def swap_cores(array):
    return lax.ppermute(array, "core", ((0, 1), (1, 0)))


def per_device(embeddings, latent, list_of, rank_of, probes):
    resident = pl.BlockSpec(memory_space=pltpu.VMEM)
    anywhere = pl.BlockSpec(memory_space=pl.ANY)
    msg_c, scaled_own, res0, w = call(
        prepare,
        (
            shape(GRP, D + 2 * SIDES, PT, dtype=BF16),
            shape(SIDES, PT, dtype=BF16),
            shape(SIDES, PT),
            shape(1, PT),
        ),
        vmem=VMEM_ALL,
        in_specs=[anywhere] * 5,
        scratch_shapes=[
            pltpu.VMEM((D, PT), BF16),
            pltpu.VMEM((1, PT), F32),
            pltpu.VMEM((1, PT), jnp.int32),
            pltpu.VMEM((1, PT), jnp.int32),
            pltpu.VMEM((SIDES - 1, PT), F32),
            pltpu.SemaphoreType.DMA((5,)),
        ],
        name="prepare",
    )(embeddings, latent[None, :], list_of[None, :], rank_of[None, :], probes)
    own_c = lax.all_to_all(msg_c, GROUP_C, 0, 0, tiled=True)
    pair = jnp.concatenate([embeddings, swap_along_z(embeddings, 1)], axis=1)
    all_r = [pair] + [swap_along_z(pair, k) for k in ORDER[2::2]]
    own_c, all_r = lax.optimization_barrier((own_c, all_r))
    other_c = swap_cores(own_c)

    place = lax.axis_index("z").astype(jnp.int32)[None]
    half_tile = [pltpu.VMEM((PIECE, ROWS), BF16)] * (PIECES // 2)
    scratch = [pltpu.VMEM((HALF, AUG), BF16), pltpu.VMEM((SIDES, HALF), BF16)]
    in_vmem = pl.BlockSpec(memory_space=pltpu.VMEM)
    in_smem = pl.BlockSpec(memory_space=pltpu.SMEM)
    part, right, *tile = call(
        first_half,
        (shape(SIDES, ROWS), shape(AUG, ROWS, dtype=BF16), *half_tile),
        in_specs=[in_vmem] * (1 + PAIRS),
        out_specs=[in_vmem] * (2 + PIECES // 2),
        scratch_shapes=scratch,
        name="first_half",
    )(own_c, *all_r)
    part, *more = call(
        second_half,
        (shape(DEPTH, SIDES, PT), *half_tile),
        in_specs=[in_smem] + [in_vmem] * 3,
        out_specs=[in_vmem] * (1 + PIECES // 2),
        scratch_shapes=scratch,
        name="second_half",
    )(place, other_c, right, part)
    tile = tile + more
    part = lax.all_to_all(part, "z", 0, 0, tiled=True)

    message, img0, weighted = call(
        first_image,
        (shape(GRP, SIDES + 8, PT), shape(SIDES, PT), shape(SIDES, PT)),
        name="first_image",
    )(part, res0, w)
    own_i = lax.all_to_all(message, GROUP_C, 0, 0, tiled=True)
    other_i = swap_cores(own_i)
    grams = block(GRP, 8, 128, at=(0, 2, 0))
    own = block(SIDES, PT)
    along_z = call(
        gram_sum,
        shape(DEPTH, 3 * SIDES, PT, dtype=BF16),
        grid=(1,),
        in_specs=[grams, grams, own, own],
        out_specs=block(DEPTH, 3 * SIDES, PT),
        name="gram_sum",
    )(own_i, other_i, scaled_own, weighted)
    along_z = lax.all_to_all(along_z, "z", 0, 0, tiled=True)

    images = block(GRP, SIDES, PT)
    scaled = block(GRP, 2 * SIDES, PT, at=(0, 2, 0))
    part, sol1, res1, dir1, gram1 = call(
        second_apply,
        (
            shape(DEPTH, SIDES + 8, PT),
            shape(SIDES, PT),
            shape(SIDES, PT),
            shape(SIDES, PT),
            shape(SIDES, SIDES),
        ),
        grid=(1,),
        in_specs=[in_smem, block(DEPTH, 3 * SIDES, PT)]
        + [images, images, scaled, scaled]
        + [own, own] + [resident] * PIECES,
        out_specs=(block(DEPTH, SIDES + 8, PT), own, own, own, block(SIDES, SIDES)),
        name="second_apply",
    )(place, along_z, own_i, other_i, own_c, other_c, res0, img0, *tile)
    part = lax.all_to_all(part, "z", 0, 0, tiled=True)

    grams, img1 = call(
        second_image, (shape(2 * GRP, 2, 128), shape(SIDES, PT)), name="second_image"
    )(part, dir1, w)
    grams = lax.all_to_all(grams, GROUP_LAST, 0, 0, tiled=True)
    return call(finish, (shape(SIDES, PT), shape(SIDES, PT)), name="finish")(
        grams, gram1, sol1, res1, dir1, img1
    )


def solution(mesh):
    grid = Mesh(mesh.devices.reshape(4, 2, 8, 4), ALL)
    in_specs = (P(None, ALL), P(ALL), P(ALL), P(ALL), P(None, ALL))
    return jax.shard_map(
        per_device,
        mesh=grid,
        in_specs=in_specs,
        out_specs=(P(None, ALL), P(None, ALL)),
        check_vma=False,
    )
```

```python
import jax
import jax.numpy as jnp
from jax import lax
from jax.experimental import pallas as pl
from jax.experimental.pallas import tpu as pltpu
from jax.sharding import Mesh
from jax.sharding import PartitionSpec as P

D = 64
SIDES = 16
LIST_LEN = 8
PT = 256
RIDGE = 0.01
GAMMA = 2.0 / D
ALL = ("y", "core", "z", "x")
GROUP_C = ("y", "x")
GROUP_LAST = ("y", "core", "x")
GRP = 16
DEPTH = 8
PAIRS = DEPTH // 2
ORDER = (0, 1, 6, 7, 2, 3, 4, 5)
HALF = GRP * PT
COLS = 2 * HALF
ROWS = DEPTH * PT
AUG = 80
VMEM_ALL = 60
PIECES = 16
PIECE = COLS // PIECES

F32 = jnp.float32
BF16 = jnp.bfloat16


def hdot(a, b, dims):
    return lax.dot_general(
        a, b, (dims, ((), ())), precision=lax.Precision.HIGHEST, preferred_element_type=F32
    )


def split3(v):
    hi = v.astype(BF16).astype(F32)
    mid = (v - hi).astype(BF16).astype(F32)
    lo = (v - hi - mid).astype(BF16).astype(F32)
    return hi, mid, lo


def spd_solve(gram, right):
    n = gram.shape[0]
    rows = lax.broadcasted_iota(jnp.int32, right.shape, 0)
    gram = 0.5 * (gram + gram.T)
    columns = [jnp.broadcast_to(gram[:, k : k + 1], right.shape) for k in range(n)]
    diagonal = jnp.ones(right.shape, F32)
    for k in range(n):
        pivot = columns[k][k : k + 1, :]
        scale = 1.0 / pivot
        factor = jnp.where(rows == k, 0.0, columns[k])
        diagonal = jnp.where(rows == k, scale, diagonal)
        for j in range(k + 1, n):
            columns[j] = columns[j] - factor * (columns[j][k : k + 1, :] * scale)
        right = right - factor * (right[k : k + 1, :] * scale)
    return right * diagonal


def prepare(
    emb_in, latent_in, list_in, rank_in, probes_in,
    msg_c, scaled_own, resid, weight,
    emb, latent, list_of, rank_of, probes, sems,
):
    pairs = (
        (latent_in, latent), (list_in, list_of), (rank_in, rank_of), (probes_in, probes), (emb_in, emb),
    )
    copies = [pltpu.make_async_copy(a, b, sems.at[i]) for i, (a, b) in enumerate(pairs)]
    for copy in copies:
        copy.start()
    for copy in copies[:3]:
        copy.wait()
    row = jnp.concatenate(
        [
            latent[...],
            list_of[...].astype(F32),
            rank_of[...].astype(F32),
            jnp.zeros((5, PT), F32),
        ],
        axis=0,
    )
    col = row.T
    same = col[:, 1:2] == row[1:2, :]
    highest = jnp.max(jnp.where(same, col[:, 0:1], -jnp.inf), axis=0, keepdims=True)
    shifted = jnp.exp(row[0:1, :] - highest)
    shifted_col = jnp.broadcast_to(shifted, (8, PT)).T[:, 0:1]
    gradient = jnp.ones((1, PT), F32)
    curvature = jnp.zeros((1, PT), F32)
    for k in range(LIST_LEN):
        held = jnp.where(col[:, 2:3] >= k, shifted_col, 0.0)
        totals = jnp.sum(jnp.where(same, held, 0.0), axis=0, keepdims=True)
        chance = shifted / totals
        active = row[2:3, :] >= k
        gradient = gradient - jnp.where(active, chance, 0.0)
        curvature = curvature + jnp.where(active, chance * (1.0 - chance), 0.0)
    w = jnp.sqrt(curvature + RIDGE)
    copies[3].wait()
    copies[4].wait()
    r0 = jnp.concatenate([gradient, probes[...]], axis=0)
    resid[...] = r0
    weight[...] = w
    scaled = w * r0
    high = scaled.astype(BF16)
    low = (scaled - high.astype(F32)).astype(BF16)
    scaled_own[...] = high
    for g in range(GRP):
        msg_c[g, :D, :] = emb[...]
        msg_c[g, D : D + SIDES, :] = high
        msg_c[g, D + SIDES :, :] = low


def norm_rows(points):
    sq = -GAMMA * jnp.sum(points * points, axis=0, keepdims=True)
    return jnp.concatenate(split3(sq), axis=0)


def half_apply(c_ref, right, tile, left, vec):
    ones = jnp.ones((3, PT), F32)
    zeros = jnp.zeros((AUG - D - 6, PT), F32)
    for g in range(GRP):
        at = slice(g * PT, (g + 1) * PT)
        points = c_ref[g, :D, :].astype(F32)
        rows = jnp.concatenate([points, ones, norm_rows(points), zeros], axis=0)
        left[at, :] = rows.astype(BF16).T
        vec[:, at] = c_ref[g, D : D + SIDES, :]
    step = 512
    total = jnp.zeros((SIDES, ROWS), F32)
    for j in range(HALF // step):
        at = slice(j * step, (j + 1) * step)
        exponent = jnp.dot(left[at, :], right[...], preferred_element_type=F32)
        kernel = jnp.exp(exponent).astype(BF16)
        tile[j * step // PIECE][pl.ds(j * step % PIECE, step), :] = kernel
        total += jnp.dot(vec[:, at], kernel, preferred_element_type=F32)
    return total


def first_half(c_ref, *more):
    r_refs, out, right, more = more[:PAIRS], more[PAIRS], more[PAIRS + 1], more[PAIRS + 2 :]
    ones = jnp.ones((3, PT), F32)
    zeros = jnp.zeros((AUG - D - 6, PT), F32)
    for k in range(DEPTH):
        points = r_refs[k // 2][:, k % 2 * PT : (k % 2 + 1) * PT].astype(F32)
        rows = [points * (2.0 * GAMMA), norm_rows(points), ones, zeros]
        right[:, k * PT : (k + 1) * PT] = jnp.concatenate(rows, axis=0).astype(BF16)
    out[...] = half_apply(c_ref, right, more[: PIECES // 2], *more[PIECES // 2 :])


def second_half(place, c_ref, right, before, out, *more):
    total = half_apply(c_ref, right, more[: PIECES // 2], *more[PIECES // 2 :])
    total = total + before[...]
    for k in range(DEPTH):
        out[lax.bitwise_xor(place[0], ORDER[k])] = total[:, k * PT : (k + 1) * PT]


def unpack(total, n):
    return jnp.concatenate(
        [total[:, 32 * n : 32 * n + 16], total[:, 32 * n + 16 : 32 * n + 32]], axis=0
    )


def first_image(parts, base, w, out, image, weighted):
    total = parts[0]
    for g in range(1, DEPTH):
        total = total + parts[g]
    r0 = base[...]
    i0 = r0 + w[...] * total
    image[...] = i0
    both = jnp.concatenate([r0, i0], axis=0)
    gram = hdot(both, both, ((1,), (1,)))
    rr, ri, ii = gram[:SIDES, :SIDES], gram[:SIDES, SIDES:], gram[SIDES:, SIDES:]
    packed = [rr[:8], rr[8:], ri[:8], ri[8:], ii[:8], ii[8:], jnp.zeros((8, 160), F32)]
    weighted[...] = w[...] * i0
    message = jnp.concatenate([w[...] * i0, jnp.concatenate(packed, axis=1)], axis=0)
    for g in range(GRP):
        out[g] = message


def gram_sum(own, other, scaled, weighted, out):
    total = own[0] + other[0]
    for g in range(1, GRP):
        total = total + (own[g] + other[g])
    high, mid, low = split3(total)
    grams = [
        jnp.concatenate([high, mid], axis=1),
        jnp.concatenate([low, jnp.zeros((8, PT - 128), F32)], axis=1),
    ]
    message = jnp.concatenate([weighted[...]] + grams, axis=0).astype(BF16)
    for g in range(DEPTH):
        out[g, :SIDES, :] = scaled[...]
        out[g, SIDES:, :] = message


def second_apply(place, along_z, own_i, other_i, own_s, other_s, *more):
    (res_ref, img_ref), more = more[:2], more[2:]
    tile, (out, sol1, res1, dir1, gram1) = more[:PIECES], more[PIECES:]
    total = along_z[0, 2 * SIDES :, :].astype(F32)
    for g in range(1, DEPTH):
        total = total + along_z[g, 2 * SIDES :, :].astype(F32)
    total = total[:8, :128] + (total[:8, 128:] + total[8:, :128])
    rr, ri, ii = unpack(total, 0), unpack(total, 1), unpack(total, 2)
    step = spd_solve(ri, rr)
    cross = hdot(step, ri, ((0,), (1,)))
    new = rr - cross - cross.T + hdot(step, hdot(ii, step, ((1,), (0,))), ((0,), (0,)))
    mix = spd_solve(rr, new)
    gram1[...] = new
    r0, i0 = res_ref[...], img_ref[...]
    sol1[...] = hdot(step, r0, ((0,), (0,)))
    r1 = r0 - hdot(step, i0, ((0,), (0,)))
    res1[...] = r1
    d1 = r1 + hdot(mix, r0, ((0,), (0,)))
    dir1[...] = d1
    rows = lax.broadcasted_iota(jnp.int32, (SIDES, SIDES), 0)
    lanes = lax.broadcasted_iota(jnp.int32, (SIDES, SIDES), 1)
    coef = jnp.concatenate([jnp.where(rows == lanes, 1.0, 0.0) + mix, -step], axis=0)
    vec = []
    for i_ref, s_ref in ((own_i, own_s), (other_i, other_s)):
        for g in range(GRP):
            wr = s_ref[g, :SIDES, :].astype(F32) + s_ref[g, SIDES:, :].astype(F32)
            both = jnp.concatenate([wr, i_ref[g]], axis=0)
            vec.append(hdot(coef, both, ((0,), (0,))).astype(BF16))
    total = jnp.zeros((SIDES, ROWS), F32)
    for j in range(PIECES):
        scaled = jnp.concatenate(vec[j * PIECE // PT : (j + 1) * PIECE // PT], axis=1)
        total += jnp.dot(scaled, tile[j][...], preferred_element_type=F32)
    weighted = []
    for k in range(DEPTH):
        both = along_z[lax.bitwise_xor(place[0], ORDER[k]), : 2 * SIDES, :].astype(F32)
        weighted.append(hdot(coef, both, ((0,), (0,))))
    gram = hdot(d1, d1, ((1,), (1,)))
    gram = gram + hdot(jnp.concatenate(weighted, axis=1), total, ((1,), (1,)))
    gram = jnp.concatenate([gram[:8], gram[8:], jnp.zeros((8, PT - 32), F32)], axis=1)
    for k in range(DEPTH):
        part = total[:, k * PT : (k + 1) * PT]
        out[lax.bitwise_xor(place[0], ORDER[k])] = jnp.concatenate([part, gram], axis=0)


def second_image(parts, base, w, out, image):
    total = parts[0]
    for g in range(1, DEPTH):
        total = total + parts[g]
    image[...] = base[...] + w[...] * total[:SIDES]
    gram = unpack(total[SIDES:], 0)
    top = jnp.concatenate([gram[i : i + 1] for i in range(8)], axis=1)
    bottom = jnp.concatenate([gram[i : i + 1] for i in range(8, 16)], axis=1)
    packed = jnp.concatenate([top, bottom], axis=0)
    out[...] = jnp.broadcast_to(packed[None], out.shape)


def finish(grams, gram1, sol1, res1, dir1, img1, sol, res):
    total = jnp.sum(grams[...], axis=0)
    gram = jnp.concatenate(
        [total[i // 8 : i // 8 + 1, 16 * (i % 8) : 16 * (i % 8) + 16] for i in range(16)], axis=0
    )
    step = spd_solve(gram, gram1[...])
    sol[...] = sol1[...] + hdot(step, dir1[...], ((0,), (0,)))
    res[...] = res1[...] - hdot(step, img1[...], ((0,), (0,)))


def shape(*dims, dtype=F32):
    return jax.ShapeDtypeStruct(dims, dtype)


def call(body, out, vmem=8, **more):
    return pl.pallas_call(
        body,
        out_shape=out,
        compiler_params=pltpu.CompilerParams(vmem_limit_bytes=int(vmem * 2**20)),
        **more,
    )


def block(*dims, at=None):
    return pl.BlockSpec(dims, lambda i: at or (0,) * len(dims))


def swap_along_z(array, k):
    return lax.ppermute(array, "z", [(i, i ^ k) for i in range(DEPTH)])


def swap_cores(array):
    return lax.ppermute(array, "core", ((0, 1), (1, 0)))


def per_device(embeddings, latent, list_of, rank_of, probes):
    resident = pl.BlockSpec(memory_space=pltpu.VMEM)
    anywhere = pl.BlockSpec(memory_space=pl.ANY)
    msg_c, scaled_own, res0, w = call(
        prepare,
        (
            shape(GRP, D + 2 * SIDES, PT, dtype=BF16),
            shape(SIDES, PT, dtype=BF16),
            shape(SIDES, PT),
            shape(1, PT),
        ),
        vmem=VMEM_ALL,
        in_specs=[anywhere] * 5,
        scratch_shapes=[
            pltpu.VMEM((D, PT), BF16),
            pltpu.VMEM((1, PT), F32),
            pltpu.VMEM((1, PT), jnp.int32),
            pltpu.VMEM((1, PT), jnp.int32),
            pltpu.VMEM((SIDES - 1, PT), F32),
            pltpu.SemaphoreType.DMA((5,)),
        ],
        name="prepare",
    )(embeddings, latent[None, :], list_of[None, :], rank_of[None, :], probes)
    own_c = lax.all_to_all(msg_c, GROUP_C, 0, 0, tiled=True)
    pair = jnp.concatenate([embeddings, swap_along_z(embeddings, 1)], axis=1)
    all_r = [pair] + [swap_along_z(pair, k) for k in ORDER[2::2]]
    own_c, all_r = lax.optimization_barrier((own_c, all_r))
    other_c = swap_cores(own_c)

    place = lax.axis_index("z").astype(jnp.int32)[None]
    half_tile = [pltpu.VMEM((PIECE, ROWS), BF16)] * (PIECES // 2)
    scratch = [pltpu.VMEM((HALF, AUG), BF16), pltpu.VMEM((SIDES, HALF), BF16)]
    in_vmem = pl.BlockSpec(memory_space=pltpu.VMEM)
    in_smem = pl.BlockSpec(memory_space=pltpu.SMEM)
    part, right, *tile = call(
        first_half,
        (shape(SIDES, ROWS), shape(AUG, ROWS, dtype=BF16), *half_tile),
        in_specs=[in_vmem] * (1 + PAIRS),
        out_specs=[in_vmem] * (2 + PIECES // 2),
        scratch_shapes=scratch,
        vmem=14,
        name="first_half",
    )(own_c, *all_r)
    part, *more = call(
        second_half,
        (shape(DEPTH, SIDES, PT), *half_tile),
        in_specs=[in_smem] + [in_vmem] * 3,
        out_specs=[in_vmem] * (1 + PIECES // 2),
        scratch_shapes=scratch,
        vmem=14,
        name="second_half",
    )(place, other_c, right, part)
    tile = tile + more
    part = lax.all_to_all(part, "z", 0, 0, tiled=True)

    message, img0, weighted = call(
        first_image,
        (shape(GRP, SIDES + 8, PT), shape(SIDES, PT), shape(SIDES, PT)),
        name="first_image",
    )(part, res0, w)
    own_i = lax.all_to_all(message, GROUP_C, 0, 0, tiled=True)
    other_i = swap_cores(own_i)
    grams = block(GRP, 8, 128, at=(0, 2, 0))
    own = block(SIDES, PT)
    along_z = call(
        gram_sum,
        shape(DEPTH, 3 * SIDES, PT, dtype=BF16),
        grid=(1,),
        in_specs=[grams, grams, own, own],
        out_specs=block(DEPTH, 3 * SIDES, PT),
        name="gram_sum",
    )(own_i, other_i, scaled_own, weighted)
    along_z = lax.all_to_all(along_z, "z", 0, 0, tiled=True)

    images = block(GRP, SIDES, PT)
    scaled = block(GRP, 2 * SIDES, PT, at=(0, 2, 0))
    part, sol1, res1, dir1, gram1 = call(
        second_apply,
        (
            shape(DEPTH, SIDES + 8, PT),
            shape(SIDES, PT),
            shape(SIDES, PT),
            shape(SIDES, PT),
            shape(SIDES, SIDES),
        ),
        grid=(1,),
        in_specs=[in_smem, block(DEPTH, 3 * SIDES, PT)]
        + [images, images, scaled, scaled]
        + [own, own] + [resident] * PIECES,
        out_specs=(block(DEPTH, SIDES + 8, PT), own, own, own, block(SIDES, SIDES)),
        name="second_apply",
    )(place, along_z, own_i, other_i, own_c, other_c, res0, img0, *tile)
    part = lax.all_to_all(part, "z", 0, 0, tiled=True)

    grams, img1 = call(
        second_image, (shape(2 * GRP, 2, 128), shape(SIDES, PT)), name="second_image"
    )(part, dir1, w)
    grams = lax.all_to_all(grams, GROUP_LAST, 0, 0, tiled=True)
    return call(finish, (shape(SIDES, PT), shape(SIDES, PT)), name="finish")(
        grams, gram1, sol1, res1, dir1, img1
    )


def solution(mesh):
    grid = Mesh(mesh.devices.reshape(4, 2, 8, 4), ALL)
    in_specs = (P(None, ALL), P(ALL), P(ALL), P(ALL), P(None, ALL))
    return jax.shard_map(
        per_device,
        mesh=grid,
        in_specs=in_specs,
        out_specs=(P(None, ALL), P(None, ALL)),
        check_vma=False,
    )
```
